512 devices in a mesh: ctx: 64 (over x, z, core), head: 8 (over y).
Axes of the slice: x: 4, y: 8, z: 8, core: 2. Of those that a mesh axis runs over, the one named last changes fastest.
Arguments:
- values: bfloat16 [8192, 4096], P('ctx', 'head'), may hold values from -6 to 6
- gate_input: bfloat16 [8192, 4096], P('ctx', 'head'), may hold values from -6 to 6
- write_proj: bfloat16 [8192, 128], P('ctx'), may hold values from -0.5 to 0.5
- read_proj: bfloat16 [8192, 128], P('ctx'), may hold values from -6 to 6
- log_decay: float32 [64, 8192], P('head', 'ctx'), may hold values from -1 to 0
- level_logit: float32 [8, 64, 8192], P(None, 'head', 'ctx'), may hold values from -8 to 2
- norm_gain: float32 [4096], P('head'), may hold values from 0.25 to 1.75
- cotangent: bfloat16 [8192, 4096], P('ctx', 'head'), may hold values from -6 to 6
- final_cotangent: float32 [64, 8192], P('head', 'ctx'), may hold values from -6 to 6
Outputs:
- mixed: bfloat16 [8192, 4096], P('ctx', 'head')
- grad_values: bfloat16 [8192, 4096], P('ctx', 'head')
- grad_gating: bfloat16 [8192, 4096], P('ctx', 'head')
- grad_write: float32 [8192, 128], P('ctx')
- grad_read: float32 [8192, 128], P('ctx')
- grad_decay: float32 [64, 8192], P('head', 'ctx')
- grad_levels: float32 [8, 64, 8192], P(None, 'head', 'ctx')
- final_state: float32 [64, 8192], P('head', 'ctx')
The draws below stay inside these ranges and needn't reach their ends.
All inputs are finite; a program needn't handle non-finite values.
Results may differ from the reference program's by a relative error of at most 0.0017.
Values sent between devices are 32-bit elements; how exact they have to be, the bound alone decides.
A program may use at most 128 MiB of HBM per device.

```python
import jax
import jax.numpy as jnp
from jax import lax

HEAD_COUNT = 64
P_SIZE = 64
N = 128
TOK_DEV = 128
BLOCK = 64
LOCAL_LEV = 1
CROSS_LEV = 6
LEVELS = 8
SEQUENCE_TOKENS = 8192
N_CTX = 64


def draw_log_decay(key, part):
    key = jax.random.fold_in(key, 17)
    random_splits = jax.random.split(key, 7)
    share_fast = 0.5
    is_fast = jax.random.uniform(random_splits[0], (HEAD_COUNT,)) < share_fast
    fast_rate = jnp.exp(jax.random.uniform(random_splits[1], (HEAD_COUNT,), minval=jnp.log(1.0 / 50.0), maxval=jnp.log(1.0 / 30.0)))
    slow_rate = 0.3 / SEQUENCE_TOKENS * jnp.exp(jax.random.uniform(random_splits[2], (HEAD_COUNT,), minval=-0.5, maxval=0.5))
    decay_speed = jnp.where(is_fast, fast_rate, slow_rate)
    shards = SEQUENCE_TOKENS // TOK_DEV
    processor_multiplier = jnp.exp(jax.random.uniform(random_splits[3], (HEAD_COUNT, shards), minval=-0.7, maxval=0.7))
    processor_multiplier = jnp.repeat(processor_multiplier, TOK_DEV, axis=1)
    jaggedness = jax.random.uniform(random_splits[4], (HEAD_COUNT, SEQUENCE_TOKENS), minval=0.5, maxval=1.5)
    spike_position = jax.random.randint(random_splits[5], (3,), 0, SEQUENCE_TOKENS)
    spike_penalty = jax.random.uniform(random_splits[6], (3, HEAD_COUNT), minval=0.2, maxval=0.4)
    spike_matches = jnp.arange(SEQUENCE_TOKENS)[None, None, :] == spike_position[:, None, None]
    spike_events = jnp.sum(jnp.where(spike_matches, jnp.log(1.0 - spike_penalty)[:, :, None], 0.0), axis=0)
    return (-decay_speed[:, None] * processor_multiplier * jaggedness + spike_events).astype(jnp.float32)


def draw_level_logit(key, part):
    key = jax.random.fold_in(key, 29)
    random_splits = jax.random.split(key, 1)
    depth = jnp.arange(LEVELS).astype(jnp.float32)
    base_level = -0.5 * (jnp.log(BLOCK * 1.0) + (depth - 1.0) * jnp.log(2.0))
    jitter = jax.random.uniform(random_splits[0], (LEVELS, HEAD_COUNT, SEQUENCE_TOKENS), minval=-0.8, maxval=0.8)
    return (base_level[:, None, None] + jitter).astype(jnp.float32)


def block_levels(stream_key, extent, cuts, low, top_value):
    level = 1.0
    for dim, parts in cuts:
        steps = jax.random.uniform(jax.random.fold_in(jax.random.fold_in(stream_key, 6), dim), (parts,), jnp.float32, low / len(cuts), top_value / len(cuts))
        level = level * jnp.repeat(jnp.exp(steps), extent[dim] // parts).reshape((-1,) + (1,) * (len(extent) - 1 - dim))
    return level


def normal_values(own_key, extent, width, most, cuts=(), held_as=jnp.bfloat16):
    loudness = block_levels(own_key, extent, cuts, -0.22, 0.18) if cuts else 1.0
    array = jax.random.normal(own_key, extent, jnp.float32) * width * loudness
    return jnp.minimum(jnp.maximum(array, -most), most).astype(held_as)


def setup_inputs(seed: int = 0) -> dict:
    key_of = jax.random.split(jax.random.key(seed), 10)
    return {
        "values": normal_values(key_of[0], (SEQUENCE_TOKENS, HEAD_COUNT * P_SIZE), 1.0, 6.0, ((0, 64), (1, 8))),
        "gate_input": normal_values(key_of[1], (SEQUENCE_TOKENS, HEAD_COUNT * P_SIZE), 1.0, 6.0, ((0, 64), (1, 8))),
        "write_proj": normal_values(key_of[2], (SEQUENCE_TOKENS, N), N ** -0.5, 0.5, ((0, 64),)),
        "read_proj": normal_values(key_of[3], (SEQUENCE_TOKENS, N), 1.0, 6.0, ((0, 64),)),
        "log_decay": draw_log_decay(jax.random.fold_in(key_of[9], 71), 0),
        "level_logit": draw_level_logit(jax.random.fold_in(key_of[9], 71), 0),
        "norm_gain": jnp.clip(1.0 + 0.15 * jax.random.normal(key_of[6], (HEAD_COUNT * P_SIZE,), jnp.float32), 0.25, 1.75),
        "cotangent": normal_values(key_of[7], (SEQUENCE_TOKENS, HEAD_COUNT * P_SIZE), 1.0, 6.0, ((0, 64), (1, 8))),
        "final_cotangent": normal_values(key_of[8], (HEAD_COUNT, N * P_SIZE), 1.0, 6.0, ((0, 8), (1, 64)), jnp.float32),
    }


epsilon = 1e-05
highest = lax.Precision.HIGHEST

def build_masks():
    positions = jnp.arange(TOK_DEV)
    is_later = positions[:, None] >= positions[None, :]
    row_block = positions[:, None] // BLOCK
    column_block = positions[None, :] // BLOCK
    level_index = (row_block != column_block).astype(jnp.int32)
    for shift_bits in range(1, LOCAL_LEV + 1):
        level_index = level_index + (row_block // 2 ** shift_bits != column_block // 2 ** shift_bits).astype(jnp.int32)
    layers = [jnp.where(is_later & (level_index == depth), 1.0, 0.0) for depth in range(LOCAL_LEV + 1)]
    return (jnp.stack(layers).astype(jnp.float32), is_later)

def local_block(value_rows, write_rows, read_rows, cumulative, weights, masks, is_later):
    scores = jnp.dot(read_rows, write_rows.T, precision=highest)
    differ = cumulative[:, :, None] - cumulative[:, None, :]
    decay = jnp.exp(jnp.where(is_later[None], differ, 0.0))
    mixing = jnp.einsum('lht,lts->hts', weights, masks, precision=highest)
    kernel = mixing * decay * scores[None]
    return jnp.einsum('hts,shp->thp', kernel, value_rows, precision=highest)

def cross_term(weight, read_rows, state):
    projected = jnp.einsum('dtn,dhnp->dthp', read_rows, state, precision=highest)
    return jnp.transpose(weight, (0, 2, 1))[..., None] * projected

def forward(values, gate_input, write_proj, read_proj, log_decay, level_logit, norm_gain, masks, is_later):
    value_rows = values.reshape(N_CTX, TOK_DEV, HEAD_COUNT, P_SIZE)
    write_rows = write_proj.reshape(N_CTX, TOK_DEV, N)
    read_rows = read_proj.reshape(N_CTX, TOK_DEV, N)
    weights = jnp.exp(level_logit).reshape(LEVELS, HEAD_COUNT, N_CTX, TOK_DEV)
    weights_dev = jnp.transpose(weights, (2, 0, 1, 3))
    cumulative = jnp.transpose(jnp.cumsum(log_decay.reshape(HEAD_COUNT, N_CTX, TOK_DEV), axis=2), (1, 0, 2))

    def one_shard(items):
        return local_block(items[0], items[1], items[2], items[3], items[4], masks, is_later)
    y_local = lax.map(jax.checkpoint(one_shard), (value_rows, write_rows, read_rows, cumulative, weights_dev[:, :LOCAL_LEV + 1]))
    totals = cumulative[:, :, -1]
    fade = jnp.exp(totals[:, :, None] - cumulative)
    faded = value_rows * jnp.transpose(fade, (0, 2, 1))[..., None]
    ends = jnp.einsum('dtn,dthp->dhnp', write_rows, faded, precision=highest)
    shard_index = jnp.arange(N_CTX)
    block, block_decay = (ends, totals)
    offset = jnp.zeros((N_CTX, HEAD_COUNT), jnp.float32)
    y_cross = jnp.zeros_like(y_local)
    step_term = jax.checkpoint(cross_term)
    for depth in range(CROSS_LEV):
        partner_index = jnp.bitwise_xor(shard_index, 2 ** depth)
        partner, partner_decay = (block[partner_index], block_decay[partner_index])
        upper = shard_index // 2 ** depth % 2 == 1
        state = jnp.where(upper[:, None, None, None], partner, 0.0)
        weight = weights_dev[:, 1 + LOCAL_LEV + depth] * jnp.exp(offset[:, :, None] + cumulative)
        y_cross = y_cross + step_term(weight, read_rows, state)
        upper_four = upper[:, None, None, None]
        block = jnp.where(upper_four, partner * jnp.exp(block_decay)[:, :, None, None] + block, block * jnp.exp(partner_decay)[:, :, None, None] + partner)
        if depth + 1 < CROSS_LEV:
            offset = offset + jnp.where(upper[:, None], partner_decay, 0.0)
        block_decay = block_decay + partner_decay
    final_state = block[0].reshape(HEAD_COUNT, N * P_SIZE) * (N / SEQUENCE_TOKENS) ** 0.5
    mixed_rows = (y_local + y_cross).reshape(SEQUENCE_TOKENS, HEAD_COUNT * P_SIZE)
    gated = mixed_rows * (gate_input * jax.nn.sigmoid(gate_input))
    mean_square = lax.optimization_barrier(jnp.sum(gated * gated, axis=1, keepdims=True)) / (HEAD_COUNT * P_SIZE)
    return (gated * lax.rsqrt(mean_square + epsilon) * norm_gain, final_state)

def reference(values, gate_input, write_proj, read_proj, log_decay, level_logit, norm_gain, cotangent, final_cotangent):
    masks, is_later = build_masks()

    def mapping(value_in, gate_in, write_in, read_in, decay_in, logit_in):
        return forward(value_in, gate_in, write_in, read_in, decay_in, logit_in, norm_gain, masks, is_later)
    outputs, pullback = jax.vjp(mapping, values.astype(jnp.float32), gate_input.astype(jnp.float32), write_proj.astype(jnp.float32), read_proj.astype(jnp.float32), log_decay, level_logit)
    grads = pullback((cotangent.astype(jnp.float32), final_cotangent))
    return (outputs[0].astype(jnp.bfloat16), grads[0].astype(jnp.bfloat16), grads[1].astype(jnp.bfloat16), grads[2], grads[3], grads[4], grads[5], outputs[1])
```

```python
import functools

import jax
import jax.numpy as jnp
from jax import lax
from jax.experimental import pallas as pl
from jax.experimental.pallas import tpu as pltpu
from jax.sharding import PartitionSpec as P

F32 = jnp.float32
BF16 = jnp.bfloat16
EPSILON = 1e-05
BLOCK = 64
FAR = -1e30
NN = (((1,), (0,)), ((), ()))
NT = (((1,), (1,)), ((), ()))
TN = (((0,), (0,)), ((), ()))


def split(array):
    high = array.astype(BF16)
    return high, (array - high.astype(F32)).astype(BF16)


def mul(a, b, dims=NN):
    return lax.dot_general(a, b, dims, preferred_element_type=F32)


def left_two(a, b, dims=NN):
    high, low = split(a)
    return mul(high, b, dims) + mul(low, b, dims)


def right_two(a, b, dims=NN):
    high, low = split(b)
    return mul(a, high, dims) + mul(a, low, dims)


def both(a, b, dims=NN):
    a_high, a_low = split(a)
    b_high, b_low = split(b)
    return mul(a_high, b_high, dims) + (mul(a_low, b_high, dims) + mul(a_high, b_low, dims))


def exact(a, b, dims=NN):
    return lax.dot_general(
        a, b, dims, precision=lax.Precision.HIGHEST, preferred_element_type=F32
    )


def iota(shape, dim):
    return lax.broadcasted_iota(jnp.int32, shape, dim)


def layer(
    sizes,
    v_ref, g_ref, b_ref, r_ref, ld_ref, ll_ref, gain_ref, ct_ref, fc_ref,
    mixed_ref, gv_ref, gg_ref, gw_ref, gr_ref, gd_ref, gl_ref, fs_ref,
    fx, fd, own_e, core_e, s1h, zr, zs, xr, xs, st,
    wx, wp, md, ya, dl, dr, d0, dh, zb, xbs, xb, g1s, g1, gsc, gvl, gsm,
    t_own, t_core, t_pair, t_z, t_plane, t_x, f_own, f_x,
    v_own, v_core, v_pair, v_z, v_plane, v_x,
    n_own, n_y, part_r, rs_r, ag_r, own_r, part_w, rs_w, ag_w, own_w,
    core_send, core_recv, z_send, z_recv, x_send, x_recv, y_send, y_recv,
    down_send, down_recv, up_send, up_recv,
):
    X, Z, Y, T, N, H, width = sizes
    C = H * width
    SR = 2 * X
    half = Z * SR
    lz, lx = Z.bit_length() - 1, X.bit_length() - 1
    cross = 1 + lz + lx
    slots = lz + lx
    final_scale = (N / (T * X * Z * 2)) ** 0.5
    channels = C * Y

    me = lax.axis_index("ctx")
    y = lax.axis_index("head")
    k = me % 2
    z = (me // 2) % Z
    x = me // (2 * Z)
    kf = k.astype(F32)

    def device(x_, z_, k_, y_):
        return (x_ * (2 * Z) + z_ * 2 + k_, y_)

    core = device(x, z, 1 - k, y)
    zs_of = [(z + j) % Z for j in range(1, Z)]
    xs_of = [(x + j) % X for j in range(1, X)]
    ys_of = [(y + j) % Y for j in range(1, Y)]
    z_dev = [device(x, p, k, y) for p in zs_of]
    x_dev = [device(p, z, k, y) for p in xs_of]
    y_dev = [device(x, z, k, p) for p in ys_of]

    barrier = pltpu.get_barrier_semaphore()
    peers = [core] + z_dev + x_dev + y_dev
    for peer in peers:
        pl.semaphore_signal(barrier, inc=1, device_id=peer, device_id_type=pl.DeviceIdType.MESH)

    sent = []

    def copy(src, dst, send_sem, recv_sem, peer):
        return pltpu.make_async_remote_copy(
            src_ref=src, dst_ref=dst, send_sem=send_sem, recv_sem=recv_sem,
            device_id=peer, device_id_type=pl.DeviceIdType.MESH,
        )

    def send(src, dst, send_sem, recv_sem, peer, cond=None):
        item = copy(src, dst, send_sem, recv_sem, peer)
        if cond is None:
            item.start()
        else:
            pl.when(cond)(item.start)
        sent.append((item, cond))

    def recv(dst, send_sem, recv_sem, peer, cond=None):
        item = copy(dst, dst, send_sem, recv_sem, peer)
        if cond is None:
            item.wait_recv()
        else:
            pl.when(cond)(item.wait_recv)

    def bit(index, place):
        return (index // 2**place) % 2 == 1

    def needs(z_, slot):
        return bit(z_, slot) if slot < lz else bit(x, slot - lz)

    def rows(start, size):
        return pl.ds(pl.multiple_of(start, size), size)

    head_of = iota((H, C), 1) // width
    pick = head_of == iota((H, C), 0)
    pick16 = jnp.where(pick, 1.0, 0.0).astype(BF16)

    def wide(tile):
        many = jnp.concatenate([tile] * (C // 128), axis=1)
        return jnp.sum(jnp.where(pick, many, 0.0), axis=0, keepdims=True)

    def spread_out(array):
        return left_two(array, pick16, TN)

    j_ = iota((N, N), 0)
    n_ = iota((N, N), 1)
    natural = ((j_ % SR) // 2) * (4 * Z) + ((j_ % half) // SR) * 4 + (j_ // half) * 2 + j_ % 2
    order = jnp.where(natural == n_, 1.0, 0.0).astype(BF16)

    write = b_ref[...]
    read = r_ref[...]
    write_p = mul(write, order, NT).astype(BF16)
    write_t = mul(order, write, NT).astype(BF16)
    read_p = mul(read, order, NT).astype(BF16)
    read_t = mul(order, read, NT).astype(BF16)

    t_row = iota((T, T), 0)
    t_col = iota((T, T), 1)
    upto = jnp.where(t_row <= t_col, 1.0, 0.0)
    cum = exact(ld_ref[...], upto)
    total = jnp.broadcast_to(cum[:, T - 1:T], (H, 128))
    t_own[...] = total
    fade = jnp.exp(cum[:, T - 1:T] - cum)
    fx[...] = spread_out(fade)
    faded = v_ref[...].astype(F32) * fx[...]
    fd[...] = faded
    own_e[...] = right_two(write_t, faded)
    f_own[...] = fc_ref[...]

    @pl.when(k == 1)
    def _():
        d0[...] = jnp.zeros((N, C), F32)

    pl.semaphore_wait(barrier, len(peers))

    send(t_own, t_core, core_send.at[0], core_recv.at[0], core)
    send(own_e, core_e, core_send.at[1], core_recv.at[1], core)
    for j, p in enumerate(xs_of):
        send(f_own, f_x.at[x], x_send.at[0, j], x_recv.at[0, x], x_dev[j])

    recv(t_core, core_send.at[0], core_recv.at[0], core)
    t_pair[...] = t_own[...] + t_core[...]
    t_z[z] = t_pair[...]
    for j, p in enumerate(zs_of):
        send(t_pair, t_z.at[z], z_send.at[0, j], z_recv.at[0, z], z_dev[j])

    scores = mul(read, write, NT)
    cum_t = jnp.transpose(jnp.concatenate(
        [cum, ll_ref[0], ll_ref[1], jnp.zeros((128 - 3 * H, T), F32)], axis=0))
    later = t_row >= t_col
    same = (t_row // BLOCK) == (t_col // BLOCK)
    lane = iota((T, 128), 1)
    left = lane < width

    def head_mix(h):
        logit = jnp.where(same, cum_t[:, H + h:H + h + 1], cum_t[:, 2 * H + h:2 * H + h + 1])
        power = cum_t[:, h:h + 1] - cum[h:h + 1, :] + logit
        return jnp.exp(jnp.where(later, power, FAR))

    def local_pair(pair):
        vals = v_ref[:, pair * 128:(pair + 1) * 128]
        zero = jnp.zeros_like(vals)
        blocks = jnp.concatenate(
            [jnp.where(left, vals, zero), jnp.where(left, zero, vals)], axis=0)
        kernels = []
        for h in (2 * pair, 2 * pair + 1):
            mix = head_mix(h)
            md[h] = mix
            kernels.append(mix * scores)
        ya[:, pair * 128:(pair + 1) * 128] = left_two(
            jnp.concatenate(kernels, axis=1), blocks)

    local_pair(0)

    recv(core_e, core_send.at[1], core_recv.at[1], core)
    upper_total = jnp.where(k == 1, t_own[...], t_core[...])
    upper_decay = wide(jnp.exp(upper_total))
    from_own = kf + (1.0 - kf) * upper_decay
    from_core = (1.0 - kf) + kf * upper_decay
    mine = rows(k * half, half)
    s1h[...] = own_e[mine, :] * from_own + core_e[mine, :] * from_core
    zr[z] = s1h[rows(z * SR, SR), :]
    for j, p in enumerate(zs_of):
        send(s1h.at[rows(p * SR, SR)], zr.at[z], z_send.at[1, j], z_recv.at[1, z], z_dev[j])

    for j, p in enumerate(zs_of):
        recv(t_z.at[p], z_send.at[0, j], z_recv.at[0, p], z_dev[j])
    tz = [[t_z[i] for i in range(Z)]]
    for i in range(lz):
        tz.append([tz[i][2 * n] + tz[i][2 * n + 1] for n in range(Z >> (i + 1))])
    t_plane[...] = tz[lz][0]
    t_x[x] = tz[lz][0]
    for j, p in enumerate(xs_of):
        send(t_plane, t_x.at[x], x_send.at[1, j], x_recv.at[1, x], x_dev[j])

    local_pair(1)

    for j, p in enumerate(zs_of):
        recv(zr.at[p], z_send.at[1, j], z_recv.at[1, p], z_dev[j])
    z_decay = [[wide(jnp.exp(tile)) for tile in level] for level in tz]
    z_nodes = [zr]
    base = 0
    for i in range(lz):
        here = z_nodes[i]
        count = Z >> (i + 1)
        there = zs.at[base:base + count]
        for n in range(count):
            there[n] = here[2 * n] * z_decay[i][2 * n + 1] + here[2 * n + 1]
        z_nodes.append(there)
        base += count

    plane = z_nodes[lz].at[0]
    xr[x] = plane[...]
    for j, p in enumerate(xs_of):
        send(plane, xr.at[x], x_send.at[2, j], x_recv.at[2, x], x_dev[j])

    def to_readers(slot, source_of):
        place = rows(k * half + z * SR, SR)
        for j, p in enumerate(zs_of):
            send(source_of(p), st.at[slot, place], down_send.at[slot, j],
                 down_recv.at[slot, z], z_dev[j], needs(p, slot))

        @pl.when(needs(z, slot))
        def _():
            st[slot, place, :] = source_of(z)[...]

    def below(nodes, i):
        return lambda p: nodes[i].at[jnp.maximum(p // 2**i - 1, 0)]

    for i in reversed(range(lz)):
        to_readers(i, below(z_nodes, i))

    local_pair(2)

    for j, p in enumerate(xs_of):
        recv(t_x.at[p], x_send.at[1, j], x_recv.at[1, p], x_dev[j])
    tx = [[t_x[i] for i in range(X)]]
    for i in range(lx):
        tx.append([tx[i][2 * n] + tx[i][2 * n + 1] for n in range(X >> (i + 1))])
    x_decay = [[wide(jnp.exp(tile)) for tile in level] for level in tx]
    for j, p in enumerate(xs_of):
        recv(xr.at[p], x_send.at[2, j], x_recv.at[2, p], x_dev[j])
    x_nodes = [xr]
    base = 0
    for i in range(lx):
        here = x_nodes[i]
        count = X >> (i + 1)
        there = xs.at[base:base + count]
        for n in range(count):
            there[n] = here[2 * n] * x_decay[i][2 * n + 1] + here[2 * n + 1]
        x_nodes.append(there)
        base += count
    for i in range(lx):
        to_readers(lz + i, lambda p, i=i: x_nodes[i].at[jnp.maximum(x // 2**i - 1, 0)])

    whole = x_nodes[lx][0] * final_scale
    slice_row = iota((SR, C), 0)
    tile_lane = iota((H, 128), 1)

    def narrow(index):
        line = jnp.sum(jnp.where(slice_row == index, whole, 0.0), axis=0, keepdims=True)
        masked = jnp.where(pick, line, 0.0)
        tile = masked[:, 0:128]
        for n in range(1, C // 128):
            tile = tile + masked[:, n * 128:(n + 1) * 128]
        return tile + pltpu.roll(tile, width, 1)

    fs_ref[...] = jnp.where(tile_lane < width, narrow(2 * x), narrow(2 * x + 1))

    offset = jnp.zeros((H, 128), F32)
    for depth in range(cross):
        wx[depth] = spread_out(jnp.exp(ll_ref[2 + depth] + (offset + cum)))
        if depth == 0:
            offset = offset + jnp.where(k == 1, t_core[...], 0.0)
        elif depth <= lz:
            i = depth - 1
            for n in range(0, Z >> i, 2):
                offset = offset + jnp.where(z // 2**i == n + 1, tz[i][n], 0.0)
        else:
            i = depth - 1 - lz
            for n in range(0, X >> i, 2):
                offset = offset + jnp.where(x // 2**i == n + 1, tx[i][n], 0.0)

    local_pair(3)

    def read_level(depth, state):
        weighted = wx[depth] * right_two(read_p, state[...])
        wp[depth] = weighted
        ya[...] = ya[...] + weighted

    @pl.when(k == 1)
    def _():
        read_level(0, core_e)

    for slot in range(slots):
        for j, p in enumerate(zs_of):
            recv(st.at[slot, rows(k * half + p * SR, SR)], down_send.at[slot, j],
                 down_recv.at[slot, p], z_dev[j], needs(z, slot))
        send(st.at[slot, mine], st.at[slot, mine], core_send.at[2 + slot],
             core_recv.at[2 + slot], core, needs(z, slot))
    other = rows((1 - k) * half, half)
    for slot in range(slots):
        recv(st.at[slot, other], core_send.at[2 + slot], core_recv.at[2 + slot], core,
             needs(z, slot))

        @pl.when(needs(z, slot))
        def _():
            read_level(1 + slot, st.at[slot])

    gate = g_ref[...].astype(F32)
    sigma = jax.nn.sigmoid(gate)
    silu = gate * sigma
    out = ya[...]
    gated = out * silu
    gain = gain_ref[...]
    scaled = ct_ref[...].astype(F32) * gain
    ones = jnp.ones((8, C), BF16)
    squares = right_two(ones, gated * gated, NT)
    inners = right_two(ones, scaled * gated, NT)
    n_own[...] = jnp.where(iota((8, T), 0) == 0, squares, inners)
    for j, p in enumerate(ys_of):
        send(n_own, n_y.at[y], y_send.at[0, j], y_recv.at[0, y], y_dev[j])
    sums = n_own[...]
    for j, p in enumerate(ys_of):
        recv(n_y.at[p], y_send.at[0, j], y_recv.at[0, p], y_dev[j])
        sums = sums + n_y[p]
    columns = jnp.transpose(jnp.concatenate([sums, jnp.zeros((120, T), F32)], axis=0))
    inverse = lax.rsqrt(columns[:, 0:1] / channels + EPSILON)
    inner = inverse * columns[:, 1:2]
    normed = gated * inverse
    mixed_ref[...] = (normed * gain).astype(BF16)
    grad_gated = inverse * (scaled - normed * (inner / channels))
    gg_ref[...] = (grad_gated * out * sigma * (1.0 + gate * (1.0 - sigma))).astype(BF16)
    grad_out = grad_gated * silu
    ya[...] = grad_out

    def state_grad(depth):
        dl[depth] = right_two(read_t, ya[...] * wx[depth])

    for slot in reversed(range(slots)):
        @pl.when(needs(z, slot))
        def _():
            state_grad(1 + slot)

        send(dl.at[1 + slot, other], dr.at[slot], core_send.at[2 + slots + slot],
             core_recv.at[2 + slots + slot], core, needs(z, slot))

    @pl.when(k == 1)
    def _():
        state_grad(0)

    send(dl.at[0], d0, core_send.at[2 + 2 * slots], core_recv.at[2 + 2 * slots], core, k == 1)

    for slot in reversed(range(slots)):
        recv(dr.at[slot], core_send.at[2 + slots + slot], core_recv.at[2 + slots + slot], core,
             needs(z, slot))

        @pl.when(needs(z, slot))
        def _():
            dh[slot] = dl[1 + slot, mine, :] + dr[slot]
            zb[z, slot] = dh[slot, rows(z * SR, SR), :]

        for j, p in enumerate(zs_of):
            send(dh.at[slot, rows(p * SR, SR)], zb.at[z, slot], up_send.at[slot, j],
                 up_recv.at[slot, z], z_dev[j], needs(z, slot))

    gsc[...] = jnp.zeros((T, T), F32)
    block_pick = jnp.where(
        iota((8, T), 0) == iota((8, T), 1) // BLOCK, 1.0, 0.0).astype(BF16)
    late = iota((1, T), 1) >= BLOCK

    def backward_pair(pair):
        cols = slice(pair * 128, (pair + 1) * 128)
        vals = v_ref[:, cols]
        grads = ya[:, cols]
        zero = jnp.zeros_like(grads)
        parts = [jnp.where(left, grads, zero), jnp.where(left, zero, grads)]
        kernels = []
        for h, part in zip((2 * pair, 2 * pair + 1), parts):
            mix = md[h]
            kernel = mix * scores
            kernels.append(kernel)
            pull = left_two(part, vals, NT)
            gsc[...] = gsc[...] + pull * mix
            pulled = pull * kernel
            sums = right_two(block_pick, pulled, NT)
            first, second = sums[0:1, :], sums[1:2, :]
            gl_ref[0, h:h + 1, :] = jnp.where(late, second, first)
            gl_ref[1, h:h + 1, :] = jnp.where(late, first, 0.0)
            gsm[h:h + 1, :] = first + second - jnp.sum(pulled, axis=0, keepdims=True)
        gvl[:, cols] = both(
            jnp.concatenate(kernels, axis=0), jnp.concatenate(parts, axis=0), TN)

    backward_pair(0)
    backward_pair(1)

    for i in range(lx):
        slot = lz + i
        for j, p in enumerate(zs_of):
            recv(zb.at[p, slot], up_send.at[slot, j], up_recv.at[slot, p], z_dev[j],
                 needs(p, slot))

        @pl.when(bit(x, i))
        def _():
            acc = zb[0, slot]
            for p in range(1, Z):
                acc = acc + zb[p, slot]
            xbs[i] = acc

        @pl.when(jnp.logical_not(bit(x, i)))
        def _():
            xbs[i] = jnp.zeros((SR, C), F32)

    for j, p in enumerate(xs_of):
        send(xbs, xb.at[x], x_send.at[3, j], x_recv.at[3, x], x_dev[j])

    backward_pair(2)
    backward_pair(3)

    part_r[...] = left_two(gsc[...], write_p)
    part_w[...] = left_two(gsc[...], read_p, TN)
    pulled_all = jnp.zeros((H, T), F32)

    def level_back(depth, state):
        weighted = ya[...] * wx[depth]
        part_r[...] = part_r[...] + both(weighted, state[...], NT)
        gl_ref[2 + depth] = right_two(pick16, ya[...] * wp[depth], NT)

    for depth in range(cross):
        cond = (k == 1) if depth == 0 else needs(z, depth - 1)

        @pl.when(cond)
        def _():
            level_back(depth, core_e if depth == 0 else st.at[depth - 1])

        @pl.when(jnp.logical_not(cond))
        def _():
            gl_ref[2 + depth] = jnp.zeros((H, T), F32)

    chunk = T // Y
    for j, p in enumerate(ys_of):
        send(part_r.at[rows(p * chunk, chunk)], rs_r.at[y], y_send.at[1, j], y_recv.at[1, y],
             y_dev[j])

    for j, p in enumerate(xs_of):
        recv(f_x.at[p], x_send.at[0, j], x_recv.at[0, p], x_dev[j])
    f_x[x] = f_own[...]
    grad = jnp.zeros((SR, C), F32)
    for n in range(X):
        tile = f_x[n]
        turned = pltpu.roll(tile, width, 1)
        grad = jnp.where(slice_row == 2 * n, wide(jnp.where(tile_lane < width, tile, turned)), grad)
        grad = jnp.where(
            slice_row == 2 * n + 1, wide(jnp.where(tile_lane < width, turned, tile)), grad)
    grad = grad * final_scale

    for j, p in enumerate(xs_of):
        recv(xb.at[p], x_send.at[3, j], x_recv.at[3, p], x_dev[j])
    xb[x] = xbs[...]
    for i in reversed(range(lx)):
        lower = grad
        for n in range(0, X >> i, 2):
            read_by = xb[(n + 1) << i, i]
            for m in range(1, 1 << i):
                read_by = read_by + xb[((n + 1) << i) + m, i]
            lower = jnp.where(x // 2**i == n, grad * x_decay[i][n + 1] + read_by, lower)
        grad = lower
    for slot in reversed(range(lz)):
        for j, p in enumerate(zs_of):
            recv(zb.at[p, slot], up_send.at[slot, j], up_recv.at[slot, p], z_dev[j],
                 needs(p, slot))
    grads = [grad]
    for i in reversed(range(lz)):
        deeper = []
        for n in range(Z >> i):
            above = grads[n // 2]
            if n % 2 == 0:
                above = above * z_decay[i][n + 1]
                for m in range(1 << i):
                    above = above + zb[((n + 1) << i) + m, i]
            deeper.append(above)
        grads = deeper
    for n in range(Z):
        g1s[n] = grads[n]
    place = rows(k * half + z * SR, SR)
    for j, p in enumerate(zs_of):
        send(g1s.at[p], g1.at[place], z_send.at[2, j], z_recv.at[2, z], z_dev[j])
    g1[place, :] = g1s[z]

    acc = part_r[rows(y * chunk, chunk), :]
    for j, p in enumerate(ys_of):
        recv(rs_r.at[p], y_send.at[1, j], y_recv.at[1, p], y_dev[j])
        acc = acc + rs_r[p]
    own_r[...] = exact(acc, order.astype(F32))
    for j, p in enumerate(ys_of):
        send(own_r, ag_r.at[y], y_send.at[2, j], y_recv.at[2, y], y_dev[j])
    ag_r[y] = own_r[...]

    for j, p in enumerate(zs_of):
        recv(g1.at[rows(k * half + p * SR, SR)], z_send.at[2, j], z_recv.at[2, p], z_dev[j])
    last = 3 + 2 * slots
    send(g1.at[mine], g1.at[mine], core_send.at[last], core_recv.at[last], core)
    recv(d0, core_send.at[last - 1], core_recv.at[last - 1], core, k == 0)
    recv(g1.at[other], core_send.at[last], core_recv.at[last], core)

    end_grad = g1[...] * from_own + d0[...]
    end_high, end_low = split(end_grad)
    spread = mul(write_p, end_high) + mul(write_p, end_low)
    faded = fd[...]
    faded_high, faded_low = split(faded)
    part_w[...] = part_w[...] + (
        mul(faded_high, end_high, NT)
        + (mul(faded_low, end_high, NT) + mul(faded_high, end_low, NT)))
    for j, p in enumerate(ys_of):
        send(part_w.at[rows(p * chunk, chunk)], rs_w.at[y], y_send.at[3, j], y_recv.at[3, y],
             y_dev[j])
    fade_pull = right_two(pick16, faded * spread, NT)
    pulled_all = gl_ref[2]
    for depth in range(1, cross):
        pulled_all = pulled_all + gl_ref[2 + depth]
    passing = jnp.sum(pulled_all, axis=1, keepdims=True)
    change = jnp.sum(fade_pull, axis=1, keepdims=True) - passing
    v_own[...] = jnp.broadcast_to(change, (H, 128))
    send(v_own, v_core, core_send.at[last + 1], core_recv.at[last + 1], core)
    gv_ref[...] = (gvl[...] + spread * fx[...]).astype(BF16)
    recv(v_core, core_send.at[last + 1], core_recv.at[last + 1], core)
    v_pair[...] = v_own[...] + v_core[...]
    for j, p in enumerate(zs_of):
        send(v_pair, v_z.at[z], z_send.at[3, j], z_recv.at[3, z], z_dev[j])

    acc = part_w[rows(y * chunk, chunk), :]
    for j, p in enumerate(ys_of):
        recv(rs_w.at[p], y_send.at[3, j], y_recv.at[3, p], y_dev[j])
        acc = acc + rs_w[p]
    own_w[...] = exact(acc, order.astype(F32))
    for j, p in enumerate(ys_of):
        send(own_w, ag_w.at[y], y_send.at[4, j], y_recv.at[4, y], y_dev[j])
    ag_w[y] = own_w[...]

    passed = jnp.where(k == 1, v_core[...], 0.0)
    for j, p in enumerate(zs_of):
        recv(v_z.at[p], z_send.at[3, j], z_recv.at[3, p], z_dev[j])
    v_z[z] = v_pair[...]
    in_plane = jnp.zeros((H, 128), F32)
    for p in range(Z):
        tile = v_z[p]
        in_plane = in_plane + tile
        passed = passed + jnp.where(z > p, tile, 0.0)
    v_plane[...] = in_plane
    for j, p in enumerate(xs_of):
        send(v_plane, v_x.at[x], x_send.at[4, j], x_recv.at[4, x], x_dev[j])
    within = exact(pulled_all + gsm[...], jnp.where(t_row >= t_col, 1.0, 0.0))
    within = within + exact(fade_pull, jnp.where(t_row < t_col, 1.0, 0.0)) - passing
    for j, p in enumerate(xs_of):
        recv(v_x.at[p], x_send.at[4, j], x_recv.at[4, p], x_dev[j])
    v_x[x] = in_plane
    for p in range(X):
        passed = passed + jnp.where(x > p, v_x[p], 0.0)
    gd_ref[...] = within + passed[:, 0:1]

    for j, p in enumerate(ys_of):
        recv(ag_r.at[p], y_send.at[2, j], y_recv.at[2, p], y_dev[j])
    for p in range(Y):
        gr_ref[p * chunk:(p + 1) * chunk, :] = ag_r[p]
    for j, p in enumerate(ys_of):
        recv(ag_w.at[p], y_send.at[4, j], y_recv.at[4, p], y_dev[j])
    for p in range(Y):
        gw_ref[p * chunk:(p + 1) * chunk, :] = ag_w[p]

    for item, cond in sent:
        if cond is None:
            item.wait_send()
        else:
            pl.when(cond)(item.wait_send)


def shards(X, Z, Y, values, gate, write, read, decay, logit, gain, cot, final_cot):
    T, C = values.shape
    N = write.shape[1]
    H = decay.shape[0]
    width = C // H
    SR = 2 * X
    half = Z * SR
    lz, lx = Z.bit_length() - 1, X.bit_length() - 1
    slots = lz + lx
    cross = 1 + slots
    chunk = T // Y

    def mem(*shape, dtype=F32):
        return pltpu.VMEM(shape, dtype)

    sem = pltpu.SemaphoreType.DMA
    scratch = dict(
        fx=mem(T, C), fd=mem(T, C), own_e=mem(N, C), core_e=mem(N, C),
        s1h=mem(half, C), zr=mem(Z, SR, C), zs=mem(Z - 1, SR, C),
        xr=mem(X, SR, C), xs=mem(X - 1, SR, C), st=mem(slots, N, C),
        wx=mem(cross, T, C), wp=mem(cross, T, C), md=mem(H, T, T), ya=mem(T, C),
        dl=mem(cross, N, C), dr=mem(slots, half, C), d0=mem(N, C), dh=mem(slots, half, C),
        zb=mem(Z, slots, SR, C), xbs=mem(lx, SR, C), xb=mem(X, lx, SR, C),
        g1s=mem(Z, SR, C), g1=mem(N, C), gsc=mem(T, T), gvl=mem(T, C), gsm=mem(H, T),
        t_own=mem(H, 128), t_core=mem(H, 128), t_pair=mem(H, 128), t_z=mem(Z, H, 128),
        t_plane=mem(H, 128), t_x=mem(X, H, 128), f_own=mem(H, 128), f_x=mem(X, H, 128),
        v_own=mem(H, 128), v_core=mem(H, 128), v_pair=mem(H, 128), v_z=mem(Z, H, 128),
        v_plane=mem(H, 128), v_x=mem(X, H, 128),
        n_own=mem(8, T), n_y=mem(Y, 8, T),
        part_r=mem(T, N), rs_r=mem(Y, chunk, N), ag_r=mem(Y, chunk, N), own_r=mem(chunk, N),
        part_w=mem(T, N), rs_w=mem(Y, chunk, N), ag_w=mem(Y, chunk, N), own_w=mem(chunk, N),
        core_send=sem((5 + 2 * slots,)), core_recv=sem((5 + 2 * slots,)),
        z_send=sem((4, Z)), z_recv=sem((4, Z)), x_send=sem((5, X)), x_recv=sem((5, X)),
        y_send=sem((5, Y)), y_recv=sem((5, Y)),
        down_send=sem((slots, Z)), down_recv=sem((slots, Z)),
        up_send=sem((slots, Z)), up_recv=sem((slots, Z)),
    )
    vmem = pl.BlockSpec(memory_space=pltpu.VMEM)
    return pl.pallas_call(
        functools.partial(layer, (X, Z, Y, T, N, H, width)),
        out_shape=(
            jax.ShapeDtypeStruct((T, C), BF16),
            jax.ShapeDtypeStruct((T, C), BF16),
            jax.ShapeDtypeStruct((T, C), BF16),
            jax.ShapeDtypeStruct((T, N), F32),
            jax.ShapeDtypeStruct((T, N), F32),
            jax.ShapeDtypeStruct((H, T), F32),
            jax.ShapeDtypeStruct(logit.shape, F32),
            jax.ShapeDtypeStruct(final_cot.shape, F32),
        ),
        in_specs=[vmem] * 9,
        out_specs=(vmem,) * 8,
        scratch_shapes=list(scratch.values()),
        compiler_params=pltpu.CompilerParams(
            collective_id=0, has_side_effects=True, vmem_limit_bytes=56 * 2**20
        ),
    )(values, gate, write, read, decay, logit, gain.reshape(1, C), cot, final_cot)


def solution(mesh):
    ctx, heads = mesh.shape["ctx"], mesh.shape["head"]
    X = 1 << ((ctx.bit_length() - 2) // 2)
    Z = ctx // 2 // X
    return jax.shard_map(
        functools.partial(shards, X, Z, heads),
        mesh=mesh,
        in_specs=(
            P("ctx", "head"),
            P("ctx", "head"),
            P("ctx", None),
            P("ctx", None),
            P("head", "ctx"),
            P(None, "head", "ctx"),
            P("head"),
            P("ctx", "head"),
            P("head", "ctx"),
        ),
        out_specs=(
            P("ctx", "head"),
            P("ctx", "head"),
            P("ctx", "head"),
            P("ctx", None),
            P("ctx", None),
            P("head", "ctx"),
            P(None, "head", "ctx"),
            P("head", "ctx"),
        ),
        check_vma=False,
    )
```

```python
import functools

import jax
import jax.numpy as jnp
from jax import lax
from jax.experimental import pallas as pl
from jax.experimental.pallas import tpu as pltpu
from jax.sharding import PartitionSpec as P

F32 = jnp.float32
BF16 = jnp.bfloat16
EPSILON = 1e-05
BLOCK = 64
FAR = -1e30
NN = (((1,), (0,)), ((), ()))
NT = (((1,), (1,)), ((), ()))
TN = (((0,), (0,)), ((), ()))


def split(array):
    high = array.astype(BF16)
    return high, (array - high.astype(F32)).astype(BF16)


def mul(a, b, dims=NN):
    return lax.dot_general(a, b, dims, preferred_element_type=F32)


def left_two(a, b, dims=NN):
    high, low = split(a)
    return mul(high, b, dims) + mul(low, b, dims)


def right_two(a, b, dims=NN):
    high, low = split(b)
    return mul(a, high, dims) + mul(a, low, dims)


def both(a, b, dims=NN):
    a_high, a_low = split(a)
    b_high, b_low = split(b)
    return mul(a_high, b_high, dims) + (mul(a_low, b_high, dims) + mul(a_high, b_low, dims))


def exact(a, b, dims=NN):
    return lax.dot_general(
        a, b, dims, precision=lax.Precision.HIGHEST, preferred_element_type=F32
    )


def left_three(a, b, dims=NN):
    high = a.astype(BF16)
    rest = a - high.astype(F32)
    middle, low = split(rest)
    return mul(high, b, dims) + (mul(middle, b, dims) + mul(low, b, dims))


def iota(shape, dim):
    return lax.broadcasted_iota(jnp.int32, shape, dim)


def far_first(count):
    return sorted(range(1, count), key=lambda j: -min(j, count - j))


def layer(
    sizes,
    v_ref, g_ref, b_ref, r_ref, ld_ref, ll_ref, gain_ref, ct_ref, fc_ref,
    mixed_ref, gv_ref, gg_ref, gw_ref, gr_ref, gd_ref, gl_ref, fs_ref,
    fx, fd, fh, fl, silu_, slope, own_e, core_e, s1h, zr, zs, xr, xs, st,
    wx, wp, md, ya, dl, dr, d0, dh, zb, d1, xbs, xb, gp, g1s, g1, gsc, gvl, gsm,
    t_own, t_core, t_pair, t_z, t_plane, t_x, f_own, f_x,
    v_own, v_core, v_pair, v_z, v_plane, v_x,
    n_own, n_y, part_r, rs_r, ag_r, own_r, part_w, rs_w, ag_w, own_w,
    core_send, core_recv, z_send, z_recv, x_send, x_recv, y_send, y_recv,
    down_send, down_recv, up_send, up_recv, pair_send, pair_recv,
):
    X, Z, Y, T, N, H, width = sizes
    C = H * width
    SR = 2 * X
    half = Z * SR
    lz, lx = Z.bit_length() - 1, X.bit_length() - 1
    cross = 1 + lz + lx
    slots = lz + lx
    final_scale = (N / (T * X * Z * 2)) ** 0.5
    channels = C * Y

    me = lax.axis_index("ctx")
    y = lax.axis_index("head")
    k = me % 2
    z = (me // 2) % Z
    x = me // (2 * Z)
    kf = k.astype(F32)

    def device(x_, z_, k_, y_):
        return (x_ * (2 * Z) + z_ * 2 + k_, y_)

    core_links = (core_send, core_recv, k, [(1 - k, device(x, z, 1 - k, y))])
    z_links = (z_send, z_recv, z, [
        (p, device(x, p, k, y)) for p in [(z + j) % Z for j in far_first(Z)]])
    down_links = (down_send, down_recv) + z_links[2:]
    up_links = (up_send, up_recv) + z_links[2:]
    x_links = (x_send, x_recv, x, [
        (p, device(p, z, k, y)) for p in [(x + j) % X for j in far_first(X)]])
    y_links = (y_send, y_recv, y, [
        (p, device(x, z, k, p)) for p in [(y + j) % Y for j in far_first(Y)]])
    z_pair = z + 1 - 2 * (z % 2)
    pair_links = (pair_send, pair_recv, 0, [(0, device(x, z_pair, k, y))])
    all_z = [(z + j) % Z for j in far_first(Z) + [0]]

    def plane_links(sends, recvs, plane):
        return (sends, recvs, z, [(p, device(plane, p, k, y)) for p in all_z])

    next_plane = x + 1 - 2 * (x % 2)
    mirror_plane = X - 1 - x

    barrier = pltpu.get_barrier_semaphore()
    peers = [dev for links in (core_links, z_links, x_links, y_links) for _, dev in links[3]]
    peers += [device(next_plane, p, k, y) for p in all_z[:-1]]
    if lx > 1:
        peers += [device(mirror_plane, p, k, y) for p in all_z[:-1]]
    for peer in peers:
        pl.semaphore_signal(barrier, inc=1, device_id=peer, device_id_type=pl.DeviceIdType.MESH)

    sent = []

    def do(cond, action):
        if cond is None:
            action()
        else:
            pl.when(cond)(action)

    def exchange(links, slot, src_of, dst_of, send_if=lambda p: None, recv_if=lambda p: None):
        send_sems, recv_sems, mine_, others = links

        def item(n, src, dst, sender):
            return pltpu.make_async_remote_copy(
                src_ref=src, dst_ref=dst, send_sem=send_sems.at[slot, n],
                recv_sem=recv_sems.at[slot, sender], device_id=others[n][1],
                device_id_type=pl.DeviceIdType.MESH,
            )

        for n, (p, _) in enumerate(others):
            out = item(n, src_of(p), dst_of(mine_), mine_)
            do(send_if(p), out.start)
            sent.append((send_if(p), out.wait_send))

        def wait():
            for n, (p, _) in enumerate(others):
                do(recv_if(p), item(n, dst_of(p), dst_of(p), p).wait_recv)

        return wait

    def bit(index, place):
        return (index // 2**place) % 2 == 1

    def needs(z_, slot):
        return bit(z_, slot) if slot < lz else bit(x, slot - lz)

    def rows(start, size):
        return pl.ds(pl.multiple_of(start, size), size)

    head_of = iota((H, C), 1) // width
    pick = head_of == iota((H, C), 0)
    pick16 = jnp.where(pick, 1.0, 0.0).astype(BF16)

    def wide(tile):
        many = jnp.concatenate([tile] * (C // 128), axis=1)
        return jnp.sum(jnp.where(pick, many, 0.0), axis=0, keepdims=True)

    def spread_out(array):
        return left_two(array, pick16, TN)

    j_ = iota((N, N), 0)
    n_ = iota((N, N), 1)
    natural = ((j_ % SR) // 2) * (4 * Z) + ((j_ % half) // SR) * 4 + (j_ // half) * 2 + j_ % 2
    order = jnp.where(natural == n_, 1.0, 0.0).astype(BF16)

    write = b_ref[...]
    read = r_ref[...]
    write_p = mul(write, order, NT).astype(BF16)
    write_t = mul(order, write, NT).astype(BF16)
    read_p = mul(read, order, NT).astype(BF16)
    read_t = mul(order, read, NT).astype(BF16)

    t_row = iota((T, T), 0)
    t_col = iota((T, T), 1)
    upto = jnp.where(t_row <= t_col, 1.0, 0.0)
    cum = exact(ld_ref[...], upto)
    total = jnp.broadcast_to(cum[:, T - 1:T], (H, 128))
    t_own[...] = total
    fade = jnp.exp(cum[:, T - 1:T] - cum)
    fx[...] = spread_out(fade)
    faded = v_ref[...].astype(F32) * fx[...]
    fd[...] = faded
    own_e[...] = right_two(write_t, faded)
    f_own[...] = fc_ref[...]

    @pl.when(k == 1)
    def _():
        d0[...] = jnp.zeros((N, C), F32)

    pl.semaphore_wait(barrier, len(peers))

    wait_total = exchange(core_links, 0, lambda p: t_own, lambda p: t_core)
    wait_end = exchange(core_links, 1, lambda p: own_e, lambda p: core_e)
    wait_final = exchange(x_links, 0, lambda p: f_own, lambda p: f_x.at[p])

    wait_total()
    t_pair[...] = t_own[...] + t_core[...]
    t_z[z] = t_pair[...]
    wait_pairs = exchange(z_links, 0, lambda p: t_pair, lambda p: t_z.at[p])

    wait_end()
    upper_total = jnp.where(k == 1, t_own[...], t_core[...])
    upper_decay = wide(jnp.exp(upper_total))
    from_own = kf + (1.0 - kf) * upper_decay
    from_core = (1.0 - kf) + kf * upper_decay
    mine = rows(k * half, half)
    s1h[...] = own_e[mine, :] * from_own + core_e[mine, :] * from_core
    wait_slices = exchange(z_links, 1, lambda p: s1h.at[rows(p * SR, SR)], lambda p: zr.at[p])
    wait_state = [None] * slots
    wait_half = [None] * slots
    wait_state[0] = exchange(
        pair_links, 0, lambda p: s1h, lambda p: st.at[0, mine],
        lambda p: z % 2 == 0, lambda p: z % 2 == 1)
    zr[z] = s1h[rows(z * SR, SR), :]

    scores = mul(read, write, NT)
    cum_t = jnp.transpose(jnp.concatenate(
        [cum, ll_ref[0], ll_ref[1], jnp.zeros((128 - 3 * H, T), F32)], axis=0))
    later = t_row >= t_col
    same = (t_row // BLOCK) == (t_col // BLOCK)
    lane = iota((T, 128), 1)
    left = lane < width

    def head_mix(h):
        logit = jnp.where(same, cum_t[:, H + h:H + h + 1], cum_t[:, 2 * H + h:2 * H + h + 1])
        power = cum_t[:, h:h + 1] - cum[h:h + 1, :] + logit
        return jnp.exp(jnp.where(later, power, FAR))

    def local_pair(pair):
        vals = v_ref[:, pair * 128:(pair + 1) * 128]
        zero = jnp.zeros_like(vals)
        blocks = jnp.concatenate(
            [jnp.where(left, vals, zero), jnp.where(left, zero, vals)], axis=0)
        kernels = []
        for h in (2 * pair, 2 * pair + 1):
            mix = head_mix(h)
            md[h] = mix
            kernels.append(mix * scores)
        ya[:, pair * 128:(pair + 1) * 128] = left_two(
            jnp.concatenate(kernels, axis=1), blocks)

    local_pair(0)

    wait_pairs()
    tz = [[t_z[i] for i in range(Z)]]
    for i in range(lz):
        tz.append([tz[i][2 * n] + tz[i][2 * n + 1] for n in range(Z >> (i + 1))])
    t_plane[...] = tz[lz][0]
    t_x[x] = tz[lz][0]
    wait_plane_totals = exchange(x_links, 1, lambda p: t_plane, lambda p: t_x.at[p])
    z_decay = [[wide(jnp.exp(tile)) for tile in level] for level in tz]

    local_pair(1)

    wait_slices()
    z_nodes = [zr]
    base = 0
    for i in range(lz):
        here = z_nodes[i]
        count = Z >> (i + 1)
        there = zs.at[base:base + count]
        for n in range(count):
            there[n] = here[2 * n] * z_decay[i][2 * n + 1] + here[2 * n + 1]
        z_nodes.append(there)
        base += count

    plane = z_nodes[lz].at[0]
    xr[x] = plane[...]
    wait_planes = exchange(x_links, 2, lambda p: plane, lambda p: xr.at[p])

    def slice_of(slot):
        return lambda p: st.at[slot, rows(k * half + p * SR, SR)]

    wait_state[lz] = exchange(
        plane_links(down_send, down_recv, next_plane), lz, lambda p: plane, slice_of(lz),
        lambda p: x % 2 == 0, lambda p: x % 2 == 1)
    for i in reversed(range(1, lz)):
        def below(p, i=i):
            return z_nodes[i].at[jnp.maximum(p // 2**i - 1, 0)]

        wait_state[i] = exchange(
            down_links, i, below, slice_of(i), lambda p, i=i: bit(p, i),
            lambda p, i=i: bit(z, i))

        @pl.when(bit(z, i))
        def _():
            st[i, rows(k * half + z * SR, SR), :] = below(z)[...]

    def from_core_too(slot):
        wait_state[slot]()
        wait_half[slot] = exchange(
            core_links, 2 + slot, lambda p: st.at[slot, mine],
            lambda p: st.at[slot, rows(p * half, half)],
            lambda p: needs(z, slot), lambda p: needs(z, slot))

    local_pair(2)
    from_core_too(0)

    wait_plane_totals()
    tx = [[t_x[i] for i in range(X)]]
    for i in range(lx):
        tx.append([tx[i][2 * n] + tx[i][2 * n + 1] for n in range(X >> (i + 1))])
    x_decay = [[wide(jnp.exp(tile)) for tile in level] for level in tx]
    wait_planes()
    x_nodes = [xr]
    base = 0
    for i in range(lx):
        here = x_nodes[i]
        count = X >> (i + 1)
        there = xs.at[base:base + count]
        for n in range(count):
            there[n] = here[2 * n] * x_decay[i][2 * n + 1] + here[2 * n + 1]
        x_nodes.append(there)
        base += count
    if lx > 1:
        lower = x_nodes[1].at[0]
        wait_cross = exchange(
            plane_links(down_send, down_recv, mirror_plane), lz + 1, lambda p: lower,
            slice_of(lz + 1), lambda p: x == 1, lambda p: x == 2)
        wait_inside = exchange(
            down_links, lz + 2, lambda p: lower, slice_of(lz + 1),
            lambda p: x == 3, lambda p: x == 3)

        @pl.when(x == 3)
        def _():
            st[lz + 1, rows(k * half + z * SR, SR), :] = lower[...]

        def wait_both():
            wait_cross()
            wait_inside()

        wait_state[lz + 1] = wait_both

    local_pair(3)

    offset = jnp.zeros((H, 128), F32)
    for depth in range(cross):
        wx[depth] = spread_out(jnp.exp(ll_ref[2 + depth] + (offset + cum)))
        if depth == 0:
            offset = offset + jnp.where(k == 1, t_core[...], 0.0)
        elif depth <= lz:
            i = depth - 1
            for n in range(0, Z >> i, 2):
                offset = offset + jnp.where(z // 2**i == n + 1, tz[i][n], 0.0)
        else:
            i = depth - 1 - lz
            for n in range(0, X >> i, 2):
                offset = offset + jnp.where(x // 2**i == n + 1, tx[i][n], 0.0)

    def read_level(depth, state):
        weighted = wx[depth] * right_two(read_p, state[...])
        wp[depth] = weighted
        ya[...] = ya[...] + weighted

    def read_slot(slot):
        wait_half[slot]()

        @pl.when(needs(z, slot))
        def _():
            read_level(1 + slot, st.at[slot])

    @pl.when(k == 1)
    def _():
        read_level(0, core_e)

    read_slot(0)

    whole = x_nodes[lx][0] * final_scale
    slice_row = iota((SR, C), 0)
    tile_lane = iota((H, 128), 1)

    def narrow(index):
        line = jnp.sum(jnp.where(slice_row == index, whole, 0.0), axis=0, keepdims=True)
        masked = jnp.where(pick, line, 0.0)
        tile = masked[:, 0:128]
        for n in range(1, C // 128):
            tile = tile + masked[:, n * 128:(n + 1) * 128]
        return tile + pltpu.roll(tile, width, 1)

    fs_ref[...] = jnp.where(tile_lane < width, narrow(2 * x), narrow(2 * x + 1))

    gate = g_ref[...].astype(F32)
    sigma = jax.nn.sigmoid(gate)
    silu_[...] = gate * sigma
    slope[...] = sigma * (1.0 + gate * (1.0 - sigma))
    faded_high, faded_low = split(fd[...])
    fh[...] = faded_high
    fl[...] = faded_low

    for slot in list(range(lz - 1, 0, -1)) + list(range(lz, slots)):
        from_core_too(slot)
        if slot < lz:
            read_slot(slot)
    for slot in range(lz, slots):
        read_slot(slot)

    silu = silu_[...]
    out = ya[...]
    gated = out * silu
    gain = gain_ref[...]
    scaled = ct_ref[...].astype(F32) * gain
    ones = jnp.ones((8, C), BF16)
    squares = right_two(ones, gated * gated, NT)
    inners = right_two(ones, scaled * gated, NT)
    n_own[...] = jnp.where(iota((8, T), 0) == 0, squares, inners)
    wait_norm = exchange(y_links, 0, lambda p: n_own, lambda p: n_y.at[p])
    wait_norm()
    n_y[y] = n_own[...]
    sums = n_y[0]
    for p in range(1, Y):
        sums = sums + n_y[p]
    columns = jnp.transpose(jnp.concatenate([sums, jnp.zeros((120, T), F32)], axis=0))
    inverse = lax.rsqrt(columns[:, 0:1] / channels + EPSILON)
    inner = inverse * columns[:, 1:2]
    normed = gated * inverse
    mixed_ref[...] = (normed * gain).astype(BF16)
    grad_gated = inverse * (scaled - normed * (inner / channels))
    gg_ref[...] = (grad_gated * out * slope[...]).astype(BF16)
    grad_out = grad_gated * silu
    ya[...] = grad_out

    def state_grad(depth):
        dl[depth] = right_two(read_t, ya[...] * wx[depth])

    wait_core_grad = [None] * slots
    wait_grad = [None] * slots
    other = rows((1 - k) * half, half)

    def start_slot(slot):
        @pl.when(needs(z, slot))
        def _():
            state_grad(1 + slot)

        wait_core_grad[slot] = exchange(
            core_links, 2 + slots + slot, lambda p: dl.at[1 + slot, rows(p * half, half)],
            lambda p: dr.at[slot], lambda p: needs(z, slot), lambda p: needs(z, slot))

    def finish_slot(slot):
        wait_core_grad[slot]()

        @pl.when(needs(z, slot))
        def _():
            dh[slot] = dl[1 + slot, mine, :] + dr[slot]

        def piece(p):
            return dh.at[slot, rows(p * SR, SR)]

        if slot == 0:
            wait_grad[0] = exchange(
                pair_links, 1, lambda p: dh.at[0], lambda p: d1,
                lambda p: z % 2 == 1, lambda p: z % 2 == 0)
        elif slot == lz:
            wait_grad[slot] = exchange(
                plane_links(up_send, up_recv, next_plane), slot, piece, lambda p: zb.at[p, slot],
                lambda p: x % 2 == 1, lambda p: x % 2 == 0)
        else:
            wait_grad[slot] = exchange(
                up_links, slot, piece, lambda p: zb.at[p, slot],
                lambda p: needs(z, slot), lambda p: needs(p, slot))

            @pl.when(needs(z, slot))
            def _():
                zb[z, slot] = piece(z)[...]

    for slot in reversed(range(slots)):
        start_slot(slot)
        if slot + 1 < slots:
            finish_slot(slot + 1)

    @pl.when(k == 1)
    def _():
        state_grad(0)

    finish_slot(0)
    wait_lowest = exchange(
        core_links, 2 + 2 * slots, lambda p: dl.at[0], lambda p: d0,
        lambda p: k == 1, lambda p: k == 0)

    gsc[...] = jnp.zeros((T, T), F32)
    block_pick = jnp.where(
        iota((8, T), 0) == iota((8, T), 1) // BLOCK, 1.0, 0.0).astype(BF16)
    late = iota((1, T), 1) >= BLOCK

    def backward_pair(pair):
        cols = slice(pair * 128, (pair + 1) * 128)
        vals = v_ref[:, cols]
        grads = ya[:, cols]
        zero = jnp.zeros_like(grads)
        parts = [jnp.where(left, grads, zero), jnp.where(left, zero, grads)]
        kernels = []
        for h, part in zip((2 * pair, 2 * pair + 1), parts):
            mix = md[h]
            kernel = mix * scores
            kernels.append(kernel)
            pull = left_two(part, vals, NT)
            gsc[...] = gsc[...] + pull * mix
            pulled = pull * kernel
            sums = right_two(block_pick, pulled, NT)
            first, second = sums[0:1, :], sums[1:2, :]
            gl_ref[0, h:h + 1, :] = jnp.where(late, second, first)
            gl_ref[1, h:h + 1, :] = jnp.where(late, first, 0.0)
            gsm[h:h + 1, :] = first + second - jnp.sum(pulled, axis=0, keepdims=True)
        gvl[:, cols] = both(
            jnp.concatenate(kernels, axis=0), jnp.concatenate(parts, axis=0), TN)

    backward_pair(0)
    backward_pair(1)

    if lx > 1:
        wait_grad[lz + 1]()

        @pl.when(x >= 2)
        def _():
            acc = zb[0, lz + 1]
            for p in range(1, Z):
                acc = acc + zb[p, lz + 1]
            xbs[...] = acc

        wait_plane_grads = exchange(
            x_links, 3, lambda p: xbs, lambda p: xb.at[p],
            lambda p: jnp.logical_and(x >= 2, p < 2), lambda p: jnp.logical_and(x < 2, p >= 2))

    backward_pair(2)
    backward_pair(3)

    part_r[...] = left_two(gsc[...], write_p)
    part_w[...] = left_two(gsc[...], read_p, TN)
    pulled_all = jnp.zeros((H, T), F32)

    def level_back(depth, state):
        weighted = ya[...] * wx[depth]
        part_r[...] = part_r[...] + both(weighted, state[...], NT)
        gl_ref[2 + depth] = right_two(pick16, ya[...] * wp[depth], NT)

    for depth in range(cross):
        cond = (k == 1) if depth == 0 else needs(z, depth - 1)

        @pl.when(cond)
        def _():
            level_back(depth, core_e if depth == 0 else st.at[depth - 1])

        @pl.when(jnp.logical_not(cond))
        def _():
            gl_ref[2 + depth] = jnp.zeros((H, T), F32)

    chunk = T // Y
    wait_read_parts = exchange(
        y_links, 1, lambda p: part_r.at[rows(p * chunk, chunk)], lambda p: rs_r.at[p])

    wait_final()
    f_x[x] = f_own[...]
    grad = jnp.zeros((SR, C), F32)
    for n in range(X):
        tile = f_x[n]
        turned = pltpu.roll(tile, width, 1)
        grad = jnp.where(slice_row == 2 * n, wide(jnp.where(tile_lane < width, tile, turned)), grad)
        grad = jnp.where(
            slice_row == 2 * n + 1, wide(jnp.where(tile_lane < width, turned, tile)), grad)
    grad = grad * final_scale

    gp[...] = grad
    if lx > 1:
        wait_plane_grads()

        @pl.when(x < 2)
        def _():
            gp[...] = gp[...] * x_decay[1][1] + (xb[2] + xb[3])

    wait_grad[lz]()

    @pl.when(x % 2 == 0)
    def _():
        upper = tx[0][1]
        for n in range(3, X, 2):
            upper = jnp.where(x == n - 1, tx[0][n], upper)
        acc = zb[0, lz]
        for p in range(1, Z):
            acc = acc + zb[p, lz]
        gp[...] = gp[...] * wide(jnp.exp(upper)) + acc

    grad = gp[...]
    for slot in reversed(range(1, lz)):
        wait_grad[slot]()
    grads = [grad]
    for i in reversed(range(lz)):
        deeper = []
        for n in range(Z >> i):
            above = grads[n // 2]
            if n % 2 == 0:
                above = above * z_decay[i][n + 1]
                for m in range(1 << i if i else 0):
                    above = above + zb[((n + 1) << i) + m, i]
            deeper.append(above)
        grads = deeper
    for n in range(Z):
        g1s[n] = grads[n]
    wait_own_grad = exchange(
        z_links, 2, lambda p: g1s.at[p], lambda p: g1.at[rows(k * half + p * SR, SR)])
    g1[rows(k * half + z * SR, SR), :] = g1s[z]

    def own_chunk(part, received, own):
        received[y] = part[rows(y * chunk, chunk), :]
        acc = received[0]
        for p in range(1, Y):
            acc = acc + received[p]
        own[...] = left_three(acc, order)

    wait_read_parts()
    own_chunk(part_r, rs_r, own_r)
    wait_read = exchange(y_links, 2, lambda p: own_r, lambda p: ag_r.at[p])
    ag_r[y] = own_r[...]

    wait_own_grad()
    wait_grad[0]()

    @pl.when(z % 2 == 0)
    def _():
        g1[mine, :] = g1[mine, :] + d1[...]

    last = 3 + 2 * slots
    wait_half_grad = exchange(
        core_links, last, lambda p: g1.at[mine], lambda p: g1.at[rows(p * half, half)])
    wait_lowest()
    wait_half_grad()

    end_grad = g1[...] * from_own + d0[...]
    end_high, end_low = split(end_grad)
    part_w[...] = part_w[...] + (
        mul(fh[...], end_high, NT) + (mul(fl[...], end_high, NT) + mul(fh[...], end_low, NT)))
    wait_write_parts = exchange(
        y_links, 3, lambda p: part_w.at[rows(p * chunk, chunk)], lambda p: rs_w.at[p])
    spread = mul(write_p, end_high) + mul(write_p, end_low)
    fade_pull = right_two(pick16, fd[...] * spread, NT)
    pulled_all = gl_ref[2]
    for depth in range(1, cross):
        pulled_all = pulled_all + gl_ref[2 + depth]
    passing = jnp.sum(pulled_all, axis=1, keepdims=True)
    change = jnp.sum(fade_pull, axis=1, keepdims=True) - passing
    v_own[...] = jnp.broadcast_to(change, (H, 128))
    wait_change = exchange(core_links, last + 1, lambda p: v_own, lambda p: v_core)
    gv_ref[...] = (gvl[...] + spread * fx[...]).astype(BF16)
    wait_change()
    v_pair[...] = v_own[...] + v_core[...]
    wait_changes = exchange(z_links, 3, lambda p: v_pair, lambda p: v_z.at[p])

    wait_write_parts()
    own_chunk(part_w, rs_w, own_w)
    wait_write = exchange(y_links, 4, lambda p: own_w, lambda p: ag_w.at[p])
    ag_w[y] = own_w[...]

    passed = jnp.where(k == 1, v_core[...], 0.0)
    wait_changes()
    v_z[z] = v_pair[...]
    in_plane = jnp.zeros((H, 128), F32)
    for p in range(Z):
        tile = v_z[p]
        in_plane = in_plane + tile
        passed = passed + jnp.where(z > p, tile, 0.0)
    v_plane[...] = in_plane
    wait_plane_changes = exchange(x_links, 4, lambda p: v_plane, lambda p: v_x.at[p])
    within = exact(pulled_all + gsm[...], jnp.where(t_row >= t_col, 1.0, 0.0))
    within = within + exact(fade_pull, jnp.where(t_row < t_col, 1.0, 0.0)) - passing
    wait_plane_changes()
    v_x[x] = in_plane
    for p in range(X):
        passed = passed + jnp.where(x > p, v_x[p], 0.0)
    gd_ref[...] = within + passed[:, 0:1]

    wait_read()
    for p in range(Y):
        gr_ref[p * chunk:(p + 1) * chunk, :] = ag_r[p]
    wait_write()
    for p in range(Y):
        gw_ref[p * chunk:(p + 1) * chunk, :] = ag_w[p]

    for cond, wait_send in sent:
        do(cond, wait_send)


def copy_out(count, *refs):
    sems = refs[2 * count]
    copies = [
        pltpu.make_async_copy(refs[n], refs[count + n], sems.at[n]) for n in range(count)
    ]
    for item in copies:
        item.start()
    for item in copies:
        item.wait()


def shards(X, Z, Y, values, gate, write, read, decay, logit, gain, cot, final_cot):
    T, C = values.shape
    N = write.shape[1]
    H = decay.shape[0]
    width = C // H
    SR = 2 * X
    half = Z * SR
    lz, lx = Z.bit_length() - 1, X.bit_length() - 1
    slots = lz + lx
    cross = 1 + slots
    chunk = T // Y

    def mem(*shape, dtype=F32):
        return pltpu.VMEM(shape, dtype)

    sem = pltpu.SemaphoreType.DMA
    scratch = dict(
        fx=mem(T, C), fd=mem(T, C), fh=mem(T, C, dtype=BF16), fl=mem(T, C, dtype=BF16),
        silu_=mem(T, C), slope=mem(T, C), own_e=mem(N, C), core_e=mem(N, C),
        s1h=mem(half, C), zr=mem(Z, SR, C), zs=mem(Z - 1, SR, C),
        xr=mem(X, SR, C), xs=mem(X - 1, SR, C), st=mem(slots, N, C),
        wx=mem(cross, T, C), wp=mem(cross, T, C), md=mem(H, T, T), ya=mem(T, C),
        dl=mem(cross, N, C), dr=mem(slots, half, C), d0=mem(N, C), dh=mem(slots, half, C),
        zb=mem(Z, slots, SR, C), d1=mem(half, C), xbs=mem(SR, C), xb=mem(X, SR, C),
        gp=mem(SR, C), g1s=mem(Z, SR, C), g1=mem(N, C), gsc=mem(T, T), gvl=mem(T, C), gsm=mem(H, T),
        t_own=mem(H, 128), t_core=mem(H, 128), t_pair=mem(H, 128), t_z=mem(Z, H, 128),
        t_plane=mem(H, 128), t_x=mem(X, H, 128), f_own=mem(H, 128), f_x=mem(X, H, 128),
        v_own=mem(H, 128), v_core=mem(H, 128), v_pair=mem(H, 128), v_z=mem(Z, H, 128),
        v_plane=mem(H, 128), v_x=mem(X, H, 128),
        n_own=mem(8, T), n_y=mem(Y, 8, T),
        part_r=mem(T, N), rs_r=mem(Y, chunk, N), ag_r=mem(Y, chunk, N), own_r=mem(chunk, N),
        part_w=mem(T, N), rs_w=mem(Y, chunk, N), ag_w=mem(Y, chunk, N), own_w=mem(chunk, N),
        core_send=sem((5 + 2 * slots, 1)), core_recv=sem((5 + 2 * slots, 2)),
        z_send=sem((4, Z)), z_recv=sem((4, Z)), x_send=sem((5, X)), x_recv=sem((5, X)),
        y_send=sem((5, Y)), y_recv=sem((5, Y)),
        down_send=sem((slots + 1, Z)), down_recv=sem((slots + 1, Z)),
        up_send=sem((slots, Z)), up_recv=sem((slots, Z)),
        pair_send=sem((2, 1)), pair_recv=sem((2, 1)),
    )
    vmem = pl.BlockSpec(memory_space=pltpu.VMEM)
    outs = (
        ((T, C), BF16), ((T, C), BF16), ((T, C), BF16), ((T, N), F32), ((T, N), F32),
        ((H, T), F32), (logit.shape, F32), (final_cot.shape, F32),
    )
    results = pl.pallas_call(
        functools.partial(layer, (X, Z, Y, T, N, H, width)),
        out_shape=tuple(jax.ShapeDtypeStruct(shape, dtype) for shape, dtype in outs),
        in_specs=[vmem] * 9,
        out_specs=(vmem,) * 8,
        scratch_shapes=list(scratch.values()),
        compiler_params=pltpu.CompilerParams(
            collective_id=0, has_side_effects=True, vmem_limit_bytes=56 * 2**20
        ),
    )(values, gate, write, read, decay, logit, gain.reshape(1, C), cot, final_cot)
    anywhere = pl.BlockSpec(memory_space=pl.ANY)
    return pl.pallas_call(
        functools.partial(copy_out, len(results)),
        out_shape=tuple(jax.ShapeDtypeStruct(shape, dtype) for shape, dtype in outs),
        in_specs=[vmem] * len(results),
        out_specs=(anywhere,) * len(results),
        scratch_shapes=[sem((len(results),))],
    )(*results)


def solution(mesh):
    ctx, heads = mesh.shape["ctx"], mesh.shape["head"]
    X = 1 << ((ctx.bit_length() - 2) // 2)
    Z = ctx // 2 // X
    return jax.shard_map(
        functools.partial(shards, X, Z, heads),
        mesh=mesh,
        in_specs=(
            P("ctx", "head"),
            P("ctx", "head"),
            P("ctx", None),
            P("ctx", None),
            P("head", "ctx"),
            P(None, "head", "ctx"),
            P("head"),
            P("ctx", "head"),
            P("head", "ctx"),
        ),
        out_specs=(
            P("ctx", "head"),
            P("ctx", "head"),
            P("ctx", "head"),
            P("ctx", None),
            P("ctx", None),
            P("head", "ctx"),
            P(None, "head", "ctx"),
            P("head", "ctx"),
        ),
        check_vma=False,
    )
```

```python
import functools

import jax
import jax.numpy as jnp
from jax import lax
from jax.experimental import pallas as pl
from jax.experimental.pallas import tpu as pltpu
from jax.sharding import PartitionSpec as P

F32 = jnp.float32
BF16 = jnp.bfloat16
EPSILON = 1e-05
BLOCK = 64
FAR = -1e30
NN = (((1,), (0,)), ((), ()))
NT = (((1,), (1,)), ((), ()))
TN = (((0,), (0,)), ((), ()))


def split(array):
    high = array.astype(BF16)
    return high, (array - high.astype(F32)).astype(BF16)


def mul(a, b, dims=NN):
    return lax.dot_general(a, b, dims, preferred_element_type=F32)


def left_two(a, b, dims=NN):
    high, low = split(a)
    return mul(high, b, dims) + mul(low, b, dims)


def right_two(a, b, dims=NN):
    high, low = split(b)
    return mul(a, high, dims) + mul(a, low, dims)


def both(a, b, dims=NN):
    a_high, a_low = split(a)
    b_high, b_low = split(b)
    return mul(a_high, b_high, dims) + (mul(a_low, b_high, dims) + mul(a_high, b_low, dims))


def exact(a, b, dims=NN):
    return lax.dot_general(
        a, b, dims, precision=lax.Precision.HIGHEST, preferred_element_type=F32
    )


def left_three(a, b, dims=NN):
    high = a.astype(BF16)
    rest = a - high.astype(F32)
    middle, low = split(rest)
    return mul(high, b, dims) + (mul(middle, b, dims) + mul(low, b, dims))


def iota(shape, dim):
    return lax.broadcasted_iota(jnp.int32, shape, dim)


def far_first(count):
    return sorted(range(1, count), key=lambda j: -min(j, count - j))


def layer(
    sizes,
    v_in, g_in, b_in, r_in, ld_in, ll_in, gain_in, ct_in, fc_in,
    mixed_out, gv_out, gg_out, gw_out, gr_out, gd_out, gl_out, fs_out,
    v_ref, g_ref, b_ref, r_ref, ld_ref, ll_ref, gain_ref, ct_ref, fc_ref,
    mixed_ref, gv_ref, gg_ref, gw_ref, gr_ref, gd_ref, gl_ref, fs_ref,
    fx, fd, fh, fl, silu_, slope, ss, s2, cols, go, own_e, core_e, s1h, zr, zs, xr, xs, st,
    wx, wp, md, ya, dl, dr, d0, dh, zb, d1, xbs, xb, gp, g1s, g1, gsc, gvl, gsm,
    t_own, t_core, t_pair, t_z, t_plane, t_x, f_own, f_x,
    v_own, v_core, v_pair, v_z, v_plane, v_x,
    n_own, n_y, part_r, rs_r, ag_r, own_r, part_w, rs_w, ag_w, own_w,
    send_sems, recv_sems, in_sems, out_sems,
):
    X, Z, Y, T, N, H, width = sizes
    C = H * width
    SR = 2 * X
    half = Z * SR
    lz, lx = Z.bit_length() - 1, X.bit_length() - 1
    cross = 1 + lz + lx
    slots = lz + lx
    final_scale = (N / (T * X * Z * 2)) ** 0.5
    channels = C * Y

    me = lax.axis_index("ctx")
    y = lax.axis_index("head")
    k = me % 2
    z = (me // 2) % Z
    x = me // (2 * Z)
    kf = k.astype(F32)

    def device(x_, z_, k_, y_):
        return (x_ * (2 * Z) + z_ * 2 + k_, y_)

    core_links = (k, [(1 - k, device(x, z, 1 - k, y))])
    z_links = (z, [(p, device(x, p, k, y)) for p in [(z + j) % Z for j in far_first(Z)]])
    x_links = (x, [(p, device(p, z, k, y)) for p in [(x + j) % X for j in far_first(X)]])
    y_links = (y, [(p, device(x, z, k, p)) for p in [(y + j) % Y for j in far_first(Y)]])
    z_pair = z + 1 - 2 * (z % 2)
    pair_links = (0, [(0, device(x, z_pair, k, y))])
    all_z = [(z + j) % Z for j in far_first(Z) + [0]]

    def plane_links(plane):
        return (z, [(p, device(plane, p, k, y)) for p in all_z])

    next_plane = x + 1 - 2 * (x % 2)
    mirror_plane = X - 1 - x

    barrier = pltpu.get_barrier_semaphore()
    peers = [dev for links in (core_links, z_links, x_links, y_links) for _, dev in links[1]]
    for peer in peers:
        pl.semaphore_signal(barrier, inc=1, device_id=peer, device_id_type=pl.DeviceIdType.MESH)

    loads = {}
    for n, (name, src, dst) in enumerate((
        ("ld", ld_in, ld_ref), ("b", b_in, b_ref), ("v", v_in, v_ref), ("fc", fc_in, fc_ref),
        ("r", r_in, r_ref), ("ll", ll_in, ll_ref), ("g", g_in, g_ref),
        ("gain", gain_in, gain_ref), ("ct", ct_in, ct_ref),
    )):
        loads[name] = pltpu.make_async_copy(src, dst, in_sems.at[n])
        loads[name].start()
    stores = []

    def store(src, dst):
        item = pltpu.make_async_copy(src, dst, out_sems.at[len(stores)])
        item.start()
        stores.append(item)

    sent = []

    def do(cond, action):
        if cond is None:
            action()
        else:
            pl.when(cond)(action)

    def exchange(links, src_of, dst_of, whole, send_if=lambda p: None, gone=None, got=None):
        mine_, others = links
        index = len(sent)
        everyone = [(None, len(others))]

        def item(src, dst, device_id):
            return pltpu.make_async_remote_copy(
                src_ref=src, dst_ref=dst, send_sem=send_sems.at[index],
                recv_sem=recv_sems.at[index], device_id=device_id,
                device_id_type=pl.DeviceIdType.MESH,
            )

        for p, device_id in others:
            do(send_if(p), item(src_of(p), dst_of(mine_), device_id).start)

        def wait_all(counts, kind):
            for cond, count in counts:
                if count:
                    ref = whole(count)
                    do(cond, getattr(item(ref, ref, others[0][1]), kind))

        sent.append(lambda: wait_all(gone or everyone, "wait_send"))

        def wait():
            wait_all(got or everyone, "wait_recv")

        return wait

    def slices(count):
        return zr.at[0:count]

    def half_of(condition):
        return [(condition, Z // 2 - 1), (jnp.logical_not(condition), Z // 2)]

    def bit(index, place):
        return (index // 2**place) % 2 == 1

    def needs(z_, slot):
        return bit(z_, slot) if slot < lz else bit(x, slot - lz)

    def rows(start, size):
        return pl.ds(pl.multiple_of(start, size), size)

    head_of = iota((H, C), 1) // width
    pick = head_of == iota((H, C), 0)
    pick16 = jnp.where(pick, 1.0, 0.0).astype(BF16)

    def wide(tile):
        many = jnp.concatenate([tile] * (C // 128), axis=1)
        return jnp.sum(jnp.where(pick, many, 0.0), axis=0, keepdims=True)

    def spread_out(array):
        return left_two(array, pick16, TN)

    j_ = iota((N, N), 0)
    n_ = iota((N, N), 1)
    natural = ((j_ % SR) // 2) * (4 * Z) + ((j_ % half) // SR) * 4 + (j_ // half) * 2 + j_ % 2
    order = jnp.where(natural == n_, 1.0, 0.0).astype(BF16)


    t_row = iota((T, T), 0)
    t_col = iota((T, T), 1)
    upto = jnp.where(t_row <= t_col, 1.0, 0.0)
    loads["ld"].wait()
    cum = exact(ld_ref[...], upto)
    total = jnp.broadcast_to(cum[:, T - 1:T], (H, 128))
    t_own[...] = total
    fade = jnp.exp(cum[:, T - 1:T] - cum)
    fx[...] = spread_out(fade)
    loads["b"].wait()
    write = b_ref[...]
    write_t = mul(order, write, NT).astype(BF16)
    loads["v"].wait()
    faded = v_ref[...].astype(F32) * fx[...]
    fd[...] = faded
    own_e[...] = right_two(write_t, faded)
    loads["fc"].wait()
    f_own[...] = fc_ref[...]

    @pl.when(k == 1)
    def _():
        d0[...] = jnp.zeros((N, C), F32)

    pl.semaphore_wait(barrier, len(peers))

    wait_total = exchange(core_links, lambda p: t_own, lambda p: t_core, lambda n: t_core)
    wait_end = exchange(core_links, lambda p: own_e, lambda p: core_e, lambda n: core_e)
    wait_final = exchange(
        x_links, lambda p: f_own, lambda p: f_x.at[p], lambda n: f_x.at[0:n])

    wait_total()
    t_pair[...] = t_own[...] + t_core[...]
    t_z[z] = t_pair[...]
    wait_pairs = exchange(
        z_links, lambda p: t_pair, lambda p: t_z.at[p], lambda n: t_z.at[0:n])

    wait_end()
    upper_total = jnp.where(k == 1, t_own[...], t_core[...])
    upper_decay = wide(jnp.exp(upper_total))
    from_own = kf + (1.0 - kf) * upper_decay
    from_core = (1.0 - kf) + kf * upper_decay
    mine = rows(k * half, half)
    s1h[...] = own_e[mine, :] * from_own + core_e[mine, :] * from_core
    wait_slices = exchange(
        z_links, lambda p: s1h.at[rows(p * SR, SR)], lambda p: zr.at[p], slices)
    wait_state = [None] * slots
    wait_half = [None] * slots
    wait_state[0] = exchange(
        pair_links, lambda p: s1h, lambda p: st.at[0, mine], lambda n: s1h,
        lambda p: z % 2 == 0, [(z % 2 == 0, 1)], [(z % 2 == 1, 1)])
    zr[z] = s1h[rows(z * SR, SR), :]

    loads["r"].wait()
    read = r_ref[...]
    write_p = mul(write, order, NT).astype(BF16)
    read_p = mul(read, order, NT).astype(BF16)
    read_t = mul(order, read, NT).astype(BF16)
    scores = mul(read, write, NT)
    loads["ll"].wait()
    cum_t = jnp.transpose(jnp.concatenate(
        [cum, ll_ref[0], ll_ref[1], jnp.zeros((128 - 3 * H, T), F32)], axis=0))
    later = t_row >= t_col
    same = (t_row // BLOCK) == (t_col // BLOCK)
    lane = iota((T, 128), 1)
    left = lane < width

    def head_mix(h):
        logit = jnp.where(same, cum_t[:, H + h:H + h + 1], cum_t[:, 2 * H + h:2 * H + h + 1])
        power = cum_t[:, h:h + 1] - cum[h:h + 1, :] + logit
        return jnp.exp(jnp.where(later, power, FAR))

    def local_pair(pair):
        vals = v_ref[:, pair * 128:(pair + 1) * 128]
        zero = jnp.zeros_like(vals)
        blocks = jnp.concatenate(
            [jnp.where(left, vals, zero), jnp.where(left, zero, vals)], axis=0)
        kernels = []
        for h in (2 * pair, 2 * pair + 1):
            mix = head_mix(h)
            md[h] = mix
            kernels.append(mix * scores)
        ya[:, pair * 128:(pair + 1) * 128] = left_two(
            jnp.concatenate(kernels, axis=1), blocks)

    local_pair(0)

    wait_pairs()
    tz = [[t_z[i] for i in range(Z)]]
    for i in range(lz):
        tz.append([tz[i][2 * n] + tz[i][2 * n + 1] for n in range(Z >> (i + 1))])
    t_plane[...] = tz[lz][0]
    t_x[x] = tz[lz][0]
    wait_plane_totals = exchange(
        x_links, lambda p: t_plane, lambda p: t_x.at[p], lambda n: t_x.at[0:n])
    z_decay = [[wide(jnp.exp(tile)) for tile in level] for level in tz]

    local_pair(1)

    wait_slices()
    z_nodes = [zr]
    base = 0
    for i in range(lz):
        here = z_nodes[i]
        count = Z >> (i + 1)
        there = zs.at[base:base + count]
        for n in range(count):
            there[n] = here[2 * n] * z_decay[i][2 * n + 1] + here[2 * n + 1]
        z_nodes.append(there)
        base += count

    plane = z_nodes[lz].at[0]
    xr[x] = plane[...]
    wait_planes = exchange(x_links, lambda p: plane, lambda p: xr.at[p], slices)

    def slice_of(slot):
        return lambda p: st.at[slot, rows(k * half + p * SR, SR)]

    wait_plane_totals()
    wait_state[lz] = exchange(
        plane_links(next_plane), lambda p: plane, slice_of(lz), slices,
        lambda p: x % 2 == 0, [(x % 2 == 0, Z)], [(x % 2 == 1, Z)])
    for i in reversed(range(1, lz)):
        def below(p, i=i):
            return z_nodes[i].at[jnp.maximum(p // 2**i - 1, 0)]

        wait_state[i] = exchange(
            z_links, below, slice_of(i), slices, lambda p: bit(p, i),
            half_of(bit(z, i)), [(bit(z, i), Z - 1)])

        @pl.when(bit(z, i))
        def _():
            st[i, rows(k * half + z * SR, SR), :] = below(z)[...]

    def from_core_too(slot):
        wait_state[slot]()
        wait_half[slot] = exchange(
            core_links, lambda p: st.at[slot, mine], lambda p: st.at[slot, rows(p * half, half)],
            lambda n: s1h, lambda p: needs(z, slot), [(needs(z, slot), 1)],
            [(needs(z, slot), 1)])

    local_pair(2)
    from_core_too(0)

    tx = [[t_x[i] for i in range(X)]]
    for i in range(lx):
        tx.append([tx[i][2 * n] + tx[i][2 * n + 1] for n in range(X >> (i + 1))])
    x_decay = [[wide(jnp.exp(tile)) for tile in level] for level in tx]
    wait_planes()
    x_nodes = [xr]
    base = 0
    for i in range(lx):
        here = x_nodes[i]
        count = X >> (i + 1)
        there = xs.at[base:base + count]
        for n in range(count):
            there[n] = here[2 * n] * x_decay[i][2 * n + 1] + here[2 * n + 1]
        x_nodes.append(there)
        base += count
    if lx > 1:
        lower = x_nodes[1].at[0]
        wait_cross = exchange(
            plane_links(mirror_plane), lambda p: lower, slice_of(lz + 1), slices,
            lambda p: x == 1, [(x == 1, Z)], [(x == 2, Z)])
        wait_inside = exchange(
            z_links, lambda p: lower, slice_of(lz + 1), slices,
            lambda p: x == 3, [(x == 3, Z - 1)], [(x == 3, Z - 1)])

        @pl.when(x == 3)
        def _():
            st[lz + 1, rows(k * half + z * SR, SR), :] = lower[...]

        def wait_both():
            wait_cross()
            wait_inside()

        wait_state[lz + 1] = wait_both

    local_pair(3)

    offset = jnp.zeros((H, 128), F32)
    for depth in range(cross):
        wx[depth] = spread_out(jnp.exp(ll_ref[2 + depth] + (offset + cum)))
        if depth == 0:
            offset = offset + jnp.where(k == 1, t_core[...], 0.0)
        elif depth <= lz:
            i = depth - 1
            for n in range(0, Z >> i, 2):
                offset = offset + jnp.where(z // 2**i == n + 1, tz[i][n], 0.0)
        else:
            i = depth - 1 - lz
            for n in range(0, X >> i, 2):
                offset = offset + jnp.where(x // 2**i == n + 1, tx[i][n], 0.0)

    def read_level(depth, state):
        weighted = wx[depth] * right_two(read_p, state[...])
        wp[depth] = weighted
        ya[...] = ya[...] + weighted

    def read_slot(slot):
        wait_half[slot]()

        @pl.when(needs(z, slot))
        def _():
            read_level(1 + slot, st.at[slot])

    @pl.when(k == 1)
    def _():
        read_level(0, core_e)

    read_slot(0)

    whole = x_nodes[lx][0] * final_scale
    slice_row = iota((SR, C), 0)
    tile_lane = iota((H, 128), 1)

    def narrow(index):
        line = jnp.sum(jnp.where(slice_row == index, whole, 0.0), axis=0, keepdims=True)
        masked = jnp.where(pick, line, 0.0)
        tile = masked[:, 0:128]
        for n in range(1, C // 128):
            tile = tile + masked[:, n * 128:(n + 1) * 128]
        return tile + pltpu.roll(tile, width, 1)

    fs_ref[...] = jnp.where(tile_lane < width, narrow(2 * x), narrow(2 * x + 1))
    store(fs_ref, fs_out)

    loads["g"].wait()
    gate = g_ref[...].astype(F32)
    sigma = jax.nn.sigmoid(gate)
    silu = gate * sigma
    silu_[...] = silu
    s2[...] = silu * silu
    loads["gain"].wait()
    loads["ct"].wait()
    ss[...] = ct_ref[...].astype(F32) * gain_ref[...] * silu
    slope[...] = sigma * (1.0 + gate * (1.0 - sigma))
    faded_high, faded_low = split(fd[...])
    fh[...] = faded_high
    fl[...] = faded_low

    for slot in list(range(lz - 1, 0, -1)) + list(range(lz, slots)):
        from_core_too(slot)
        if slot < lz:
            read_slot(slot)
    for slot in range(lz, slots):
        read_slot(slot)

    out = ya[...]

    def folded(array):
        tile = array[:, 0:128]
        for n in range(1, C // 128):
            tile = tile + array[:, n * 128:(n + 1) * 128]
        return tile

    ones = jnp.ones((8, 128), BF16)
    squares = right_two(ones, folded(out * out * s2[...]), NT)
    inners = right_two(ones, folded(out * ss[...]), NT)
    n_own[...] = jnp.where(iota((8, T), 0) == 0, squares, inners)
    wait_norm = exchange(
        y_links, lambda p: n_own, lambda p: n_y.at[p], lambda n: n_y.at[0:n])
    n_y[y] = n_own[...]
    wait_norm()
    sums = n_y[0]
    for p in range(1, Y):
        sums = sums + n_y[p]
    inverse = lax.rsqrt(sums[0:1, :] / channels + EPSILON)
    turn = inverse * inverse * (inverse * sums[1:2, :] / channels)
    cols[...] = jnp.transpose(
        jnp.concatenate([inverse, turn, jnp.zeros((126, T), F32)], axis=0))
    go[...] = cols[:, 0:1] * ss[...] - cols[:, 1:2] * (out * s2[...])

    def state_grad(depth):
        dl[depth] = right_two(read_t, go[...] * wx[depth])

    wait_core_grad = [None] * slots
    wait_grad = [None] * slots
    other = rows((1 - k) * half, half)

    def start_slot(slot):
        @pl.when(needs(z, slot))
        def _():
            state_grad(1 + slot)

        wait_core_grad[slot] = exchange(
            core_links, lambda p: dl.at[1 + slot, rows(p * half, half)], lambda p: dr.at[slot],
            lambda n: s1h, lambda p: needs(z, slot), [(needs(z, slot), 1)],
            [(needs(z, slot), 1)])

    def finish_slot(slot):
        wait_core_grad[slot]()

        @pl.when(needs(z, slot))
        def _():
            dh[slot] = dl[1 + slot, mine, :] + dr[slot]

        def piece(p):
            return dh.at[slot, rows(p * SR, SR)]

        if slot == 0:
            wait_grad[0] = exchange(
                pair_links, lambda p: dh.at[0], lambda p: d1, lambda n: s1h,
                lambda p: z % 2 == 1, [(z % 2 == 1, 1)], [(z % 2 == 0, 1)])
        elif slot == lz:
            wait_grad[slot] = exchange(
                plane_links(next_plane), piece, lambda p: zb.at[p, slot], slices,
                lambda p: x % 2 == 1, [(x % 2 == 1, Z)], [(x % 2 == 0, Z)])
        else:
            wait_grad[slot] = exchange(
                z_links, piece, lambda p: zb.at[p, slot], slices,
                lambda p: needs(z, slot), [(needs(z, slot), Z - 1)],
                half_of(bit(z, slot)) if slot < lz else [(needs(z, slot), Z - 1)])

            @pl.when(needs(z, slot))
            def _():
                zb[z, slot] = piece(z)[...]

    for slot in reversed(range(slots)):
        start_slot(slot)
        if slot + 1 < slots:
            finish_slot(slot + 1)

    @pl.when(k == 1)
    def _():
        state_grad(0)

    finish_slot(0)
    wait_lowest = exchange(
        core_links, lambda p: dl.at[0], lambda p: d0, lambda n: core_e,
        lambda p: k == 1, [(k == 1, 1)], [(k == 0, 1)])

    inverse, turn = cols[:, 0:1], cols[:, 1:2]
    gated = ya[...] * silu_[...]
    gain = gain_ref[...]
    mixed_ref[...] = (gated * inverse * gain).astype(BF16)
    store(mixed_ref, mixed_out)
    grad_gated = inverse * (ct_ref[...].astype(F32) * gain) - turn * gated
    gg_ref[...] = (grad_gated * ya[...] * slope[...]).astype(BF16)
    store(gg_ref, gg_out)

    gsc[...] = jnp.zeros((T, T), F32)
    block_pick = jnp.where(
        iota((8, T), 0) == iota((8, T), 1) // BLOCK, 1.0, 0.0).astype(BF16)
    late = iota((1, T), 1) >= BLOCK

    def backward_pair(pair):
        lanes = slice(pair * 128, (pair + 1) * 128)
        vals = v_ref[:, lanes]
        grads = go[:, lanes]
        zero = jnp.zeros_like(grads)
        parts = [jnp.where(left, grads, zero), jnp.where(left, zero, grads)]
        kernels = []
        for h, part in zip((2 * pair, 2 * pair + 1), parts):
            mix = md[h]
            kernel = mix * scores
            kernels.append(kernel)
            pull = left_two(part, vals, NT)
            gsc[...] = gsc[...] + pull * mix
            pulled = pull * kernel
            sums = right_two(block_pick, pulled, NT)
            first, second = sums[0:1, :], sums[1:2, :]
            gl_ref[0, h:h + 1, :] = jnp.where(late, second, first)
            gl_ref[1, h:h + 1, :] = jnp.where(late, first, 0.0)
            gsm[h:h + 1, :] = first + second - jnp.sum(pulled, axis=0, keepdims=True)
        gvl[:, lanes] = both(
            jnp.concatenate(kernels, axis=0), jnp.concatenate(parts, axis=0), TN)

    backward_pair(0)
    backward_pair(1)

    if lx > 1:
        wait_grad[lz + 1]()

        @pl.when(x >= 2)
        def _():
            acc = zb[0, lz + 1]
            for p in range(1, Z):
                acc = acc + zb[p, lz + 1]
            xbs[...] = acc

        wait_plane_grads = exchange(
            x_links, lambda p: xbs, lambda p: xb.at[p], slices,
            lambda p: jnp.logical_and(x >= 2, p < 2), [(x >= 2, 2)], [(x < 2, 2)])

    backward_pair(2)
    backward_pair(3)

    part_r[...] = left_two(gsc[...], write_p)
    part_w[...] = left_two(gsc[...], read_p, TN)
    pulled_all = jnp.zeros((H, T), F32)

    def level_back(depth, state):
        weighted = go[...] * wx[depth]
        part_r[...] = part_r[...] + both(weighted, state[...], NT)
        gl_ref[2 + depth] = right_two(pick16, go[...] * wp[depth], NT)

    for depth in range(cross):
        cond = (k == 1) if depth == 0 else needs(z, depth - 1)

        @pl.when(cond)
        def _():
            level_back(depth, core_e if depth == 0 else st.at[depth - 1])

        @pl.when(jnp.logical_not(cond))
        def _():
            gl_ref[2 + depth] = jnp.zeros((H, T), F32)

    store(gl_ref, gl_out)

    chunk = T // Y
    wait_read_parts = exchange(
        y_links, lambda p: part_r.at[rows(p * chunk, chunk)], lambda p: rs_r.at[p],
        lambda n: rs_r.at[0:n])

    wait_final()
    f_x[x] = f_own[...]
    grad = jnp.zeros((SR, C), F32)
    for n in range(X):
        tile = f_x[n]
        turned = pltpu.roll(tile, width, 1)
        grad = jnp.where(slice_row == 2 * n, wide(jnp.where(tile_lane < width, tile, turned)), grad)
        grad = jnp.where(
            slice_row == 2 * n + 1, wide(jnp.where(tile_lane < width, turned, tile)), grad)
    grad = grad * final_scale

    gp[...] = grad
    if lx > 1:
        wait_plane_grads()

        @pl.when(x < 2)
        def _():
            gp[...] = gp[...] * x_decay[1][1] + (xb[2] + xb[3])

    wait_grad[lz]()

    @pl.when(x % 2 == 0)
    def _():
        upper = tx[0][1]
        for n in range(3, X, 2):
            upper = jnp.where(x == n - 1, tx[0][n], upper)
        acc = zb[0, lz]
        for p in range(1, Z):
            acc = acc + zb[p, lz]
        gp[...] = gp[...] * wide(jnp.exp(upper)) + acc

    grad = gp[...]
    for slot in reversed(range(1, lz)):
        wait_grad[slot]()
    grads = [grad]
    for i in reversed(range(lz)):
        deeper = []
        for n in range(Z >> i):
            above = grads[n // 2]
            if n % 2 == 0:
                above = above * z_decay[i][n + 1]
                for m in range(1 << i if i else 0):
                    above = above + zb[((n + 1) << i) + m, i]
            deeper.append(above)
        grads = deeper
    for n in range(Z):
        g1s[n] = grads[n]
    wait_own_grad = exchange(
        z_links, lambda p: g1s.at[p], lambda p: g1.at[rows(k * half + p * SR, SR)], slices)
    g1[rows(k * half + z * SR, SR), :] = g1s[z]

    def own_chunk(part, received, own):
        received[y] = part[rows(y * chunk, chunk), :]
        acc = received[0]
        for p in range(1, Y):
            acc = acc + received[p]
        own[...] = left_three(acc, order)

    wait_read_parts()
    own_chunk(part_r, rs_r, own_r)
    wait_read = exchange(
        y_links, lambda p: own_r, lambda p: ag_r.at[p], lambda n: ag_r.at[0:n])
    ag_r[y] = own_r[...]

    wait_own_grad()
    wait_grad[0]()

    @pl.when(z % 2 == 0)
    def _():
        g1[mine, :] = g1[mine, :] + d1[...]

    wait_half_grad = exchange(
        core_links, lambda p: g1.at[mine], lambda p: g1.at[rows(p * half, half)],
        lambda n: s1h)
    wait_lowest()
    wait_half_grad()

    end_grad = g1[...] * from_own + d0[...]
    pulled_all = gl_ref[2]
    for depth in range(1, cross):
        pulled_all = pulled_all + gl_ref[2 + depth]
    passing = jnp.sum(pulled_all, axis=1, keepdims=True)
    line = jnp.sum(own_e[...] * end_grad, axis=0, keepdims=True)
    change = jnp.sum(jnp.where(pick, line, 0.0), axis=1, keepdims=True) - passing
    v_own[...] = jnp.broadcast_to(change, (H, 128))
    wait_change = exchange(core_links, lambda p: v_own, lambda p: v_core, lambda n: v_core)
    end_high, end_low = split(end_grad)
    part_w[...] = part_w[...] + (
        mul(fh[...], end_high, NT) + (mul(fl[...], end_high, NT) + mul(fh[...], end_low, NT)))
    wait_write_parts = exchange(
        y_links, lambda p: part_w.at[rows(p * chunk, chunk)], lambda p: rs_w.at[p],
        lambda n: rs_w.at[0:n])
    wait_change()
    v_pair[...] = v_own[...] + v_core[...]
    wait_changes = exchange(
        z_links, lambda p: v_pair, lambda p: v_z.at[p], lambda n: v_z.at[0:n])
    spread = mul(write_p, end_high) + mul(write_p, end_low)
    gv_ref[...] = (gvl[...] + spread * fx[...]).astype(BF16)
    store(gv_ref, gv_out)
    fade_pull = right_two(pick16, fd[...] * spread, NT)
    within = exact(pulled_all + gsm[...], jnp.where(t_row >= t_col, 1.0, 0.0))
    within = within + exact(fade_pull, jnp.where(t_row < t_col, 1.0, 0.0)) - passing
    wait_read()
    for p in range(Y):
        gr_ref[p * chunk:(p + 1) * chunk, :] = ag_r[p]
    store(gr_ref, gr_out)

    wait_write_parts()
    own_chunk(part_w, rs_w, own_w)
    wait_write = exchange(
        y_links, lambda p: own_w, lambda p: ag_w.at[p], lambda n: ag_w.at[0:n])
    ag_w[y] = own_w[...]

    passed = jnp.where(k == 1, v_core[...], 0.0)
    wait_changes()
    v_z[z] = v_pair[...]
    in_plane = jnp.zeros((H, 128), F32)
    for p in range(Z):
        tile = v_z[p]
        in_plane = in_plane + tile
        passed = passed + jnp.where(z > p, tile, 0.0)
    v_plane[...] = in_plane
    wait_plane_changes = exchange(
        x_links, lambda p: v_plane, lambda p: v_x.at[p], lambda n: v_x.at[0:n])
    wait_plane_changes()
    v_x[x] = in_plane
    for p in range(X):
        passed = passed + jnp.where(x > p, v_x[p], 0.0)
    gd_ref[...] = within + passed[:, 0:1]
    store(gd_ref, gd_out)
    wait_write()
    for p in range(Y):
        gw_ref[p * chunk:(p + 1) * chunk, :] = ag_w[p]
    store(gw_ref, gw_out)
    for item in stores:
        item.wait()

    for wait_sent in sent:
        wait_sent()


def copy_out(count, *refs):
    sems = refs[2 * count]
    copies = [
        pltpu.make_async_copy(refs[n], refs[count + n], sems.at[n]) for n in range(count)
    ]
    for item in copies:
        item.start()
    for item in copies:
        item.wait()


def shards(X, Z, Y, values, gate, write, read, decay, logit, gain, cot, final_cot):
    T, C = values.shape
    N = write.shape[1]
    H = decay.shape[0]
    width = C // H
    SR = 2 * X
    half = Z * SR
    lz, lx = Z.bit_length() - 1, X.bit_length() - 1
    slots = lz + lx
    cross = 1 + slots
    chunk = T // Y

    def mem(*shape, dtype=F32):
        return pltpu.VMEM(shape, dtype)

    sem = pltpu.SemaphoreType.DMA
    outs = (
        ((T, C), BF16), ((T, C), BF16), ((T, C), BF16), ((T, N), F32), ((T, N), F32),
        ((H, T), F32), (logit.shape, F32), (final_cot.shape, F32),
    )
    args = (values, gate, write, read, decay, logit, gain.reshape(1, C), cot, final_cot)
    scratch = dict(
        fx=mem(T, C), fd=mem(T, C), fh=mem(T, C, dtype=BF16), fl=mem(T, C, dtype=BF16),
        silu_=mem(T, C), slope=mem(T, C), ss=mem(T, C), s2=mem(T, C), cols=mem(T, 128),
        go=mem(T, C), own_e=mem(N, C), core_e=mem(N, C),
        s1h=mem(half, C), zr=mem(Z, SR, C), zs=mem(Z - 1, SR, C),
        xr=mem(X, SR, C), xs=mem(X - 1, SR, C), st=mem(slots, N, C),
        wx=mem(cross, T, C), wp=mem(cross, T, C), md=mem(H, T, T), ya=mem(T, C),
        dl=mem(cross, N, C), dr=mem(slots, half, C), d0=mem(N, C), dh=mem(slots, half, C),
        zb=mem(Z, slots, SR, C), d1=mem(half, C), xbs=mem(SR, C), xb=mem(X, SR, C),
        gp=mem(SR, C), g1s=mem(Z, SR, C), g1=mem(N, C), gsc=mem(T, T), gvl=mem(T, C), gsm=mem(H, T),
        t_own=mem(H, 128), t_core=mem(H, 128), t_pair=mem(H, 128), t_z=mem(Z, H, 128),
        t_plane=mem(H, 128), t_x=mem(X, H, 128), f_own=mem(H, 128), f_x=mem(X, H, 128),
        v_own=mem(H, 128), v_core=mem(H, 128), v_pair=mem(H, 128), v_z=mem(Z, H, 128),
        v_plane=mem(H, 128), v_x=mem(X, H, 128),
        n_own=mem(8, T), n_y=mem(Y, 8, T),
        part_r=mem(T, N), rs_r=mem(Y, chunk, N), ag_r=mem(Y, chunk, N), own_r=mem(chunk, N),
        part_w=mem(T, N), rs_w=mem(Y, chunk, N), ag_w=mem(Y, chunk, N), own_w=mem(chunk, N),
        send_sems=sem((24 + 4 * slots,)), recv_sems=sem((24 + 4 * slots,)),
        in_sems=sem((9,)), out_sems=sem((8,)),
    )
    vmem = pl.BlockSpec(memory_space=pltpu.VMEM)
    anywhere = pl.BlockSpec(memory_space=pl.ANY)
    results = pl.pallas_call(
        functools.partial(layer, (X, Z, Y, T, N, H, width)),
        out_shape=tuple(jax.ShapeDtypeStruct(shape, dtype) for shape, dtype in outs),
        in_specs=[anywhere] * len(args),
        out_specs=(anywhere,) * len(outs),
        scratch_shapes=(
            [mem(*a.shape, dtype=a.dtype) for a in args]
            + [mem(*shape, dtype=dtype) for shape, dtype in outs] + list(scratch.values())),
        compiler_params=pltpu.CompilerParams(
            collective_id=0, has_side_effects=True, vmem_limit_bytes=56 * 2**20
        ),
    )(*args)
    return pl.pallas_call(
        functools.partial(copy_out, len(results)),
        out_shape=tuple(jax.ShapeDtypeStruct(shape, dtype) for shape, dtype in outs),
        in_specs=[vmem] * len(results),
        out_specs=(anywhere,) * len(results),
        scratch_shapes=[sem((len(results),))],
    )(*results)


def solution(mesh):
    ctx, heads = mesh.shape["ctx"], mesh.shape["head"]
    X = 1 << ((ctx.bit_length() - 2) // 2)
    Z = ctx // 2 // X
    return jax.shard_map(
        functools.partial(shards, X, Z, heads),
        mesh=mesh,
        in_specs=(
            P("ctx", "head"),
            P("ctx", "head"),
            P("ctx", None),
            P("ctx", None),
            P("head", "ctx"),
            P(None, "head", "ctx"),
            P("head"),
            P("ctx", "head"),
            P("head", "ctx"),
        ),
        out_specs=(
            P("ctx", "head"),
            P("ctx", "head"),
            P("ctx", "head"),
            P("ctx", None),
            P("ctx", None),
            P("head", "ctx"),
            P(None, "head", "ctx"),
            P("head", "ctx"),
        ),
        check_vma=False,
    )
```

```python
import functools

import jax
import jax.numpy as jnp
from jax import lax
from jax.experimental import pallas as pl
from jax.experimental.pallas import tpu as pltpu
from jax.sharding import PartitionSpec as P

F32 = jnp.float32
BF16 = jnp.bfloat16
EPSILON = 1e-05
BLOCK = 64
FAR = -1e30
NN = (((1,), (0,)), ((), ()))
NT = (((1,), (1,)), ((), ()))
TN = (((0,), (0,)), ((), ()))


def split(array):
    high = array.astype(BF16)
    return high, (array - high.astype(F32)).astype(BF16)


def mul(a, b, dims=NN):
    return lax.dot_general(a, b, dims, preferred_element_type=F32)


def left_two(a, b, dims=NN):
    high, low = split(a)
    return mul(high, b, dims) + mul(low, b, dims)


def right_two(a, b, dims=NN):
    high, low = split(b)
    return mul(a, high, dims) + mul(a, low, dims)


def both(a, b, dims=NN):
    a_high, a_low = split(a)
    b_high, b_low = split(b)
    return mul(a_high, b_high, dims) + (mul(a_low, b_high, dims) + mul(a_high, b_low, dims))


def exact(a, b, dims=NN):
    return lax.dot_general(
        a, b, dims, precision=lax.Precision.HIGHEST, preferred_element_type=F32
    )


def left_three(a, b, dims=NN):
    high = a.astype(BF16)
    rest = a - high.astype(F32)
    middle, low = split(rest)
    return mul(high, b, dims) + (mul(middle, b, dims) + mul(low, b, dims))


def iota(shape, dim):
    return lax.broadcasted_iota(jnp.int32, shape, dim)


def far_first(count):
    return sorted(range(1, count), key=lambda j: -min(j, count - j))


def layer(
    sizes,
    v_in, g_in, b_in, r_in, ld_in, ll_in, gain_in, ct_in, fc_in,
    mixed_out, gv_out, gg_out, gw_out, gr_out, gd_out, gl_out, fs_out,
    v_ref, g_ref, b_ref, r_ref, ld_ref, ll_ref, gain_ref, ct_ref, fc_ref,
    mixed_ref, gv_ref, gg_ref, gw_ref, gr_ref, gd_ref, gl_ref, fs_ref,
    fx, fd, fh, fl, silu_, slope, ss, s2, cols, go, rt, gh, gl2, own_e, core_e, s1h, s1t, zr, zs, plane_t, xr, xs, st,
    wx, wp, md, ya, dl, dr, d0, dh, zb, d1, xbs, xb, gp, g1s, g1, gsc, gvl, gsm,
    t_own, t_core, f_own, f_x,
    v_own, v_core, v_pair, v_z, v_plane, v_x,
    n_own, n_y, part_r, rs_r, own_r, part_w, rs_w, own_w,
    send_sems, recv_sems, in_sems, out_sems,
):
    X, Z, Y, T, N, H, width = sizes
    C = H * width
    SR = 2 * X
    half = Z * SR
    lz, lx = Z.bit_length() - 1, X.bit_length() - 1
    cross = 1 + lz + lx
    slots = lz + lx
    final_scale = (N / (T * X * Z * 2)) ** 0.5
    channels = C * Y

    me = lax.axis_index("ctx")
    y = lax.axis_index("head")
    k = me % 2
    z = (me // 2) % Z
    x = me // (2 * Z)
    kf = k.astype(F32)

    def device(x_, z_, k_, y_):
        return (x_ * (2 * Z) + z_ * 2 + k_, y_)

    core_links = (k, [(1 - k, device(x, z, 1 - k, y))])
    z_links = (z, [(p, device(x, p, k, y)) for p in [(z + j) % Z for j in far_first(Z)]])
    x_links = (x, [(p, device(p, z, k, y)) for p in [(x + j) % X for j in far_first(X)]])
    y_links = (y, [(p, device(x, z, k, p)) for p in [(y + j) % Y for j in far_first(Y)]])
    z_pair = z + 1 - 2 * (z % 2)
    pair_links = (0, [(0, device(x, z_pair, k, y))])
    all_z = [(z + j) % Z for j in far_first(Z) + [0]]

    def plane_links(plane):
        return (z, [(p, device(plane, p, k, y)) for p in all_z])

    next_plane = x + 1 - 2 * (x % 2)
    mirror_plane = X - 1 - x

    barrier = pltpu.get_barrier_semaphore()
    peers = [dev for links in (core_links, z_links, x_links, y_links) for _, dev in links[1]]
    for peer in peers:
        pl.semaphore_signal(barrier, inc=1, device_id=peer, device_id_type=pl.DeviceIdType.MESH)

    loads = {}
    for n, (name, src, dst) in enumerate((
        ("ld", ld_in, ld_ref), ("b", b_in, b_ref), ("v", v_in, v_ref), ("fc", fc_in, fc_ref),
        ("r", r_in, r_ref), ("ll", ll_in, ll_ref), ("g", g_in, g_ref),
        ("gain", gain_in, gain_ref), ("ct", ct_in, ct_ref),
    )):
        loads[name] = pltpu.make_async_copy(src, dst, in_sems.at[n])
        loads[name].start()
    stores = []

    def store(src, dst):
        item = pltpu.make_async_copy(src, dst, out_sems.at[len(stores)])
        item.start()
        stores.append(item)

    sent = []

    def do(cond, action):
        if cond is None:
            action()
        else:
            pl.when(cond)(action)

    def exchange(links, src_of, dst_of, whole, send_if=lambda p: None, gone=None, got=None):
        mine_, others = links
        index = len(sent)
        everyone = [(None, len(others))]

        def item(src, dst, device_id):
            return pltpu.make_async_remote_copy(
                src_ref=src, dst_ref=dst, send_sem=send_sems.at[index],
                recv_sem=recv_sems.at[index], device_id=device_id,
                device_id_type=pl.DeviceIdType.MESH,
            )

        for p, device_id in others:
            do(send_if(p), item(src_of(p), dst_of(mine_), device_id).start)

        def wait_all(counts, kind):
            for cond, count in counts:
                if count:
                    ref = whole(count)
                    do(cond, getattr(item(ref, ref, others[0][1]), kind))

        sent.append(lambda: wait_all(gone or everyone, "wait_send"))

        def wait():
            wait_all(got or everyone, "wait_recv")

        return wait

    def slices(count):
        return g1s.at[0:count]

    def half_of(condition):
        return [(condition, Z // 2 - 1), (jnp.logical_not(condition), Z // 2)]

    def bit(index, place):
        return (index // 2**place) % 2 == 1

    def needs(z_, slot):
        return bit(z_, slot) if slot < lz else bit(x, slot - lz)

    def rows(start, size):
        return pl.ds(pl.multiple_of(start, size), size)

    head_of = iota((H, C), 1) // width
    pick = head_of == iota((H, C), 0)
    pick16 = jnp.where(pick, 1.0, 0.0).astype(BF16)

    def wide(tile):
        many = jnp.concatenate([tile] * (C // 128), axis=1)
        return jnp.sum(jnp.where(pick, many, 0.0), axis=0, keepdims=True)

    def spread_out(array):
        return left_two(array, pick16, TN)

    j_ = iota((N, N), 0)
    n_ = iota((N, N), 1)
    natural = ((j_ % SR) // 2) * (4 * Z) + ((j_ % half) // SR) * 4 + (j_ // half) * 2 + j_ % 2
    order = jnp.where(natural == n_, 1.0, 0.0).astype(BF16)


    t_row = iota((T, T), 0)
    t_col = iota((T, T), 1)
    upto = jnp.where(t_row <= t_col, 1.0, 0.0)
    loads["ld"].wait()
    cum = exact(ld_ref[...], upto)
    total = jnp.broadcast_to(cum[:, T - 1:T], (H, 128))
    t_own[...] = total
    fade = jnp.exp(cum[:, T - 1:T] - cum)
    fx[...] = spread_out(fade)
    loads["b"].wait()
    write = b_ref[...]
    write_t = mul(order, write, NT).astype(BF16)
    loads["v"].wait()
    faded = v_ref[...].astype(F32) * fx[...]
    fd[...] = faded
    own_e[...] = right_two(write_t, faded)
    loads["fc"].wait()
    f_own[...] = fc_ref[...]

    @pl.when(k == 1)
    def _():
        d0[...] = jnp.zeros((N, C), F32)

    pl.semaphore_wait(barrier, len(peers))

    wait_total = exchange(core_links, lambda p: t_own, lambda p: t_core, lambda n: t_core)
    wait_end = exchange(
        core_links, lambda p: own_e.at[rows(p * half, half)],
        lambda p: core_e.at[rows((1 - p) * half, half)], lambda n: s1h)
    wait_total()
    upper_total = jnp.where(k == 1, t_own[...], t_core[...])
    upper_decay = wide(jnp.exp(upper_total))
    from_own = kf + (1.0 - kf) * upper_decay
    from_core = (1.0 - kf) + kf * upper_decay
    mine = rows(k * half, half)
    chip_total = t_own[...] + t_core[...]
    for n in range(Z):
        s1t[n, :, C:] = chip_total

    wait_end()
    merged = own_e[mine, :] * from_own + core_e[mine, :] * from_core
    for n in range(Z):
        s1t[n, :, :C] = merged[n * SR:(n + 1) * SR, :]
    wait_slices = exchange(
        z_links, lambda p: s1t.at[p], lambda p: zr.at[p], lambda n: zr.at[0:n])
    s1h[...] = merged
    wait_state = [None] * slots
    wait_half = [None] * slots
    wait_final = exchange(
        x_links, lambda p: f_own, lambda p: f_x.at[p], lambda n: f_x.at[0:n])
    wait_state[0] = exchange(
        pair_links, lambda p: s1h, lambda p: st.at[0, mine], lambda n: s1h,
        lambda p: z % 2 == 0, [(z % 2 == 0, 1)], [(z % 2 == 1, 1)])
    zr[z] = s1t[z]
    wait_other_end = exchange(
        core_links, lambda p: own_e.at[0:half], lambda p: core_e.at[0:half], lambda n: s1h,
        lambda p: k == 0, [(k == 0, 1)], [(k == 1, 1)])

    loads["r"].wait()
    read = r_ref[...]
    write_p = mul(write, order, NT).astype(BF16)
    read_p = mul(read, order, NT).astype(BF16)
    read_t = mul(order, read, NT).astype(BF16)
    rt[...] = read_t
    scores = mul(read, write, NT)
    loads["ll"].wait()
    cum_t = jnp.transpose(jnp.concatenate(
        [cum, ll_ref[0], ll_ref[1], jnp.zeros((128 - 3 * H, T), F32)], axis=0))
    later = t_row >= t_col
    same = (t_row // BLOCK) == (t_col // BLOCK)
    lane = iota((T, 128), 1)
    left = lane < width

    def head_mix(h):
        logit = jnp.where(same, cum_t[:, H + h:H + h + 1], cum_t[:, 2 * H + h:2 * H + h + 1])
        power = cum_t[:, h:h + 1] - cum[h:h + 1, :] + logit
        return jnp.exp(jnp.where(later, power, FAR))

    def local_pair(pair):
        vals = v_ref[:, pair * 128:(pair + 1) * 128]
        zero = jnp.zeros_like(vals)
        blocks = jnp.concatenate(
            [jnp.where(left, vals, zero), jnp.where(left, zero, vals)], axis=0)
        kernels = []
        for h in (2 * pair, 2 * pair + 1):
            mix = head_mix(h)
            md[h] = mix
            kernels.append(mix * scores)
        ya[:, pair * 128:(pair + 1) * 128] = left_two(
            jnp.concatenate(kernels, axis=1), blocks)

    local_pair(0)

    local_pair(1)

    wait_slices()

    def tree_totals(tiles):
        levels = [tiles]
        while len(levels[-1]) > 1:
            last = levels[-1]
            levels.append([last[n] + last[n + 1] for n in range(0, len(last), 2)])
        decays = [
            [wide(jnp.exp(tile)) if n % 2 else None for n, tile in enumerate(level)]
            for level in levels[:-1]]
        return levels, decays

    tz, z_decay = tree_totals([zr[n, :, C:] for n in range(Z)])
    z_nodes = [zr]
    base = 0
    for i in range(lz):
        here = z_nodes[i]
        count = Z >> (i + 1)
        there = zs.at[base:base + count]
        for n in range(count):
            there[n] = here[2 * n, :, :C] * z_decay[i][2 * n + 1] + here[2 * n + 1, :, :C]
        z_nodes.append(there)
        base += count

    plane = z_nodes[lz].at[0]
    plane_t[:, :C] = plane[...]
    plane_t[:, C:] = tz[lz][0]
    wait_planes = exchange(
        x_links, lambda p: plane_t, lambda p: xr.at[p], lambda n: xr.at[0:n])
    xr[x] = plane_t[...]

    def slice_of(slot):
        return lambda p: st.at[slot, rows(k * half + p * SR, SR)]

    wait_final()
    wait_state[lz] = exchange(
        plane_links(next_plane), lambda p: plane, slice_of(lz), slices,
        lambda p: x % 2 == 0, [(x % 2 == 0, Z)], [(x % 2 == 1, Z)])
    for i in reversed(range(1, lz)):
        def below(p, i=i):
            return z_nodes[i].at[jnp.maximum(p // 2**i - 1, 0)]

        wait_state[i] = exchange(
            z_links, below, slice_of(i), slices, lambda p: bit(p, i),
            half_of(bit(z, i)), [(bit(z, i), Z - 1)])

        @pl.when(bit(z, i))
        def _():
            st[i, rows(k * half + z * SR, SR), :] = below(z)[...]

    def from_core_too(slot):
        wait_state[slot]()
        wait_half[slot] = exchange(
            core_links, lambda p: st.at[slot, mine], lambda p: st.at[slot, rows(p * half, half)],
            lambda n: s1h, lambda p: needs(z, slot), [(needs(z, slot), 1)],
            [(needs(z, slot), 1)])

    local_pair(2)
    from_core_too(0)

    wait_planes()
    tx, x_decay = tree_totals([xr[n, :, C:] for n in range(X)])
    x_nodes = [xr]
    base = 0
    for i in range(lx):
        here = x_nodes[i]
        count = X >> (i + 1)
        there = xs.at[base:base + count]
        for n in range(count):
            there[n] = here[2 * n, :, :C] * x_decay[i][2 * n + 1] + here[2 * n + 1, :, :C]
        x_nodes.append(there)
        base += count
    if lx > 1:
        lower = x_nodes[1].at[0]
        wait_cross = exchange(
            plane_links(mirror_plane), lambda p: lower, slice_of(lz + 1), slices,
            lambda p: x == 1, [(x == 1, Z)], [(x == 2, Z)])
        wait_inside = exchange(
            z_links, lambda p: lower, slice_of(lz + 1), slices,
            lambda p: x == 3, [(x == 3, Z - 1)], [(x == 3, Z - 1)])

        @pl.when(x == 3)
        def _():
            st[lz + 1, rows(k * half + z * SR, SR), :] = lower[...]

        def wait_both():
            wait_cross()
            wait_inside()

        wait_state[lz + 1] = wait_both

    local_pair(3)

    offset = jnp.zeros((H, 128), F32)
    for depth in range(cross):
        wx[depth] = spread_out(jnp.exp(ll_ref[2 + depth] + (offset + cum)))
        if depth == 0:
            offset = offset + jnp.where(k == 1, t_core[...], 0.0)
        elif depth <= lz:
            i = depth - 1
            for n in range(0, Z >> i, 2):
                offset = offset + jnp.where(z // 2**i == n + 1, tz[i][n], 0.0)
        else:
            i = depth - 1 - lz
            for n in range(0, X >> i, 2):
                offset = offset + jnp.where(x // 2**i == n + 1, tx[i][n], 0.0)

    def read_level(depth, state):
        weighted = wx[depth] * right_two(read_p, state[...])
        wp[depth] = weighted
        ya[...] = ya[...] + weighted

    def read_slot(slot):
        wait_half[slot]()

        @pl.when(needs(z, slot))
        def _():
            read_level(1 + slot, st.at[slot])

    wait_other_end()

    @pl.when(k == 1)
    def _():
        read_level(0, core_e)

    read_slot(0)

    whole = x_nodes[lx][0] * final_scale
    slice_row = iota((SR, C), 0)
    tile_lane = iota((H, 128), 1)

    def narrow(index):
        line = jnp.sum(jnp.where(slice_row == index, whole, 0.0), axis=0, keepdims=True)
        masked = jnp.where(pick, line, 0.0)
        tile = masked[:, 0:128]
        for n in range(1, C // 128):
            tile = tile + masked[:, n * 128:(n + 1) * 128]
        return tile + pltpu.roll(tile, width, 1)

    fs_ref[...] = jnp.where(tile_lane < width, narrow(2 * x), narrow(2 * x + 1))
    store(fs_ref, fs_out)

    loads["g"].wait()
    gate = g_ref[...].astype(F32)
    sigma = jax.nn.sigmoid(gate)
    silu = gate * sigma
    silu_[...] = silu
    s2[...] = silu * silu
    loads["gain"].wait()
    loads["ct"].wait()
    ss[...] = ct_ref[...].astype(F32) * gain_ref[...] * silu
    slope[...] = sigma * (1.0 + gate * (1.0 - sigma))
    faded_high, faded_low = split(fd[...])
    fh[...] = faded_high
    fl[...] = faded_low

    for slot in list(range(lz - 1, 0, -1)) + list(range(lz, slots)):
        from_core_too(slot)
        if slot < lz:
            read_slot(slot)
    for slot in range(lz, slots):
        read_slot(slot)

    out = ya[...]

    def folded(array):
        tile = array[:, 0:128]
        for n in range(1, C // 128):
            tile = tile + array[:, n * 128:(n + 1) * 128]
        return tile

    ones = jnp.ones((8, 128), BF16)
    squares = right_two(ones, folded(out * out * s2[...]), NT)
    inners = right_two(ones, folded(out * ss[...]), NT)
    n_own[...] = jnp.where(iota((8, T), 0) == 0, squares, inners)
    wait_norm = exchange(
        y_links, lambda p: n_own, lambda p: n_y.at[p], lambda n: n_y.at[0:n])
    n_y[y] = n_own[...]
    wait_norm()
    sums = n_y[0]
    for p in range(1, Y):
        sums = sums + n_y[p]
    inverse = lax.rsqrt(sums[0:1, :] / channels + EPSILON)
    turn = inverse * inverse * (inverse * sums[1:2, :] / channels)
    cols[...] = jnp.transpose(
        jnp.concatenate([inverse, turn, jnp.zeros((126, T), F32)], axis=0))
    go[...] = cols[:, 0:1] * ss[...] - cols[:, 1:2] * (out * s2[...])

    def state_grad(depth):
        dl[depth] = right_two(read_t, go[...] * wx[depth])

    def half_grad(depth, part):
        read_half = rt[part, :]
        dl[depth, part, :] = mul(read_half, gh[...]) + mul(read_half, gl2[...])

    wait_core_grad = [None] * slots
    wait_grad = [None] * slots
    other = rows((1 - k) * half, half)

    def start_slot(slot):
        @pl.when(needs(z, slot))
        def _():
            high, low = split(go[...] * wx[1 + slot])
            gh[...] = high
            gl2[...] = low
            half_grad(1 + slot, other)

        wait_core_grad[slot] = exchange(
            core_links, lambda p: dl.at[1 + slot, rows(p * half, half)], lambda p: dr.at[slot],
            lambda n: s1h, lambda p: needs(z, slot), [(needs(z, slot), 1)],
            [(needs(z, slot), 1)])

        @pl.when(needs(z, slot))
        def _():
            half_grad(1 + slot, mine)

    def finish_slot(slot):
        wait_core_grad[slot]()

        @pl.when(needs(z, slot))
        def _():
            dh[slot] = dl[1 + slot, mine, :] + dr[slot]

        def piece(p):
            return dh.at[slot, rows(p * SR, SR)]

        if slot == 0:
            wait_grad[0] = exchange(
                pair_links, lambda p: dh.at[0], lambda p: d1, lambda n: s1h,
                lambda p: z % 2 == 1, [(z % 2 == 1, 1)], [(z % 2 == 0, 1)])
        elif slot == lz:
            wait_grad[slot] = exchange(
                plane_links(next_plane), piece, lambda p: zb.at[p, slot], slices,
                lambda p: x % 2 == 1, [(x % 2 == 1, Z)], [(x % 2 == 0, Z)])
        else:
            wait_grad[slot] = exchange(
                z_links, piece, lambda p: zb.at[p, slot], slices,
                lambda p: needs(z, slot), [(needs(z, slot), Z - 1)],
                half_of(bit(z, slot)) if slot < lz else [(needs(z, slot), Z - 1)])

            @pl.when(needs(z, slot))
            def _():
                zb[z, slot] = piece(z)[...]

    for slot in reversed(range(slots)):
        start_slot(slot)
        if slot + 1 < slots:
            finish_slot(slot + 1)

    @pl.when(k == 1)
    def _():
        state_grad(0)

    finish_slot(0)
    wait_lowest = exchange(
        core_links, lambda p: dl.at[0], lambda p: d0, lambda n: core_e,
        lambda p: k == 1, [(k == 1, 1)], [(k == 0, 1)])

    inverse, turn = cols[:, 0:1], cols[:, 1:2]
    gated = ya[...] * silu_[...]
    gain = gain_ref[...]
    mixed_ref[...] = (gated * inverse * gain).astype(BF16)
    store(mixed_ref, mixed_out)
    grad_gated = inverse * (ct_ref[...].astype(F32) * gain) - turn * gated
    gg_ref[...] = (grad_gated * ya[...] * slope[...]).astype(BF16)
    store(gg_ref, gg_out)

    gsc[...] = jnp.zeros((T, T), F32)
    block_pick = jnp.where(
        iota((8, T), 0) == iota((8, T), 1) // BLOCK, 1.0, 0.0).astype(BF16)
    late = iota((1, T), 1) >= BLOCK

    def backward_pair(pair):
        lanes = slice(pair * 128, (pair + 1) * 128)
        vals = v_ref[:, lanes]
        grads = go[:, lanes]
        zero = jnp.zeros_like(grads)
        parts = [jnp.where(left, grads, zero), jnp.where(left, zero, grads)]
        kernels = []
        for h, part in zip((2 * pair, 2 * pair + 1), parts):
            mix = md[h]
            kernel = mix * scores
            kernels.append(kernel)
            pull = left_two(part, vals, NT)
            gsc[...] = gsc[...] + pull * mix
            pulled = pull * kernel
            sums = right_two(block_pick, pulled, NT)
            first, second = sums[0:1, :], sums[1:2, :]
            gl_ref[0, h:h + 1, :] = jnp.where(late, second, first)
            gl_ref[1, h:h + 1, :] = jnp.where(late, first, 0.0)
            gsm[h:h + 1, :] = first + second - jnp.sum(pulled, axis=0, keepdims=True)
        gvl[:, lanes] = both(
            jnp.concatenate(kernels, axis=0), jnp.concatenate(parts, axis=0), TN)

    backward_pair(0)
    backward_pair(1)

    if lx > 1:
        wait_grad[lz + 1]()

        @pl.when(x >= 2)
        def _():
            acc = zb[0, lz + 1]
            for p in range(1, Z):
                acc = acc + zb[p, lz + 1]
            xbs[...] = acc

        wait_plane_grads = exchange(
            x_links, lambda p: xbs, lambda p: xb.at[p], slices,
            lambda p: jnp.logical_and(x >= 2, p < 2), [(x >= 2, 2)], [(x < 2, 2)])

    backward_pair(2)
    backward_pair(3)

    part_r[...] = left_two(gsc[...], write_p)
    part_w[...] = left_two(gsc[...], read_p, TN)
    pulled_all = jnp.zeros((H, T), F32)

    def level_back(depth, state):
        weighted = go[...] * wx[depth]
        part_r[...] = part_r[...] + both(weighted, state[...], NT)
        gl_ref[2 + depth] = right_two(pick16, go[...] * wp[depth], NT)

    for depth in range(cross):
        cond = (k == 1) if depth == 0 else needs(z, depth - 1)

        @pl.when(cond)
        def _():
            level_back(depth, core_e if depth == 0 else st.at[depth - 1])

        @pl.when(jnp.logical_not(cond))
        def _():
            gl_ref[2 + depth] = jnp.zeros((H, T), F32)

    store(gl_ref, gl_out)

    chunk = T // Y
    wait_read_parts = exchange(
        y_links, lambda p: part_r.at[rows(p * chunk, chunk)], lambda p: rs_r.at[p],
        lambda n: rs_r.at[0:n])

    f_x[x] = f_own[...]
    grad = jnp.zeros((SR, C), F32)
    for n in range(X):
        tile = f_x[n]
        turned = pltpu.roll(tile, width, 1)
        grad = jnp.where(slice_row == 2 * n, wide(jnp.where(tile_lane < width, tile, turned)), grad)
        grad = jnp.where(
            slice_row == 2 * n + 1, wide(jnp.where(tile_lane < width, turned, tile)), grad)
    grad = grad * final_scale

    gp[...] = grad
    if lx > 1:
        wait_plane_grads()

        @pl.when(x < 2)
        def _():
            gp[...] = gp[...] * x_decay[1][1] + (xb[2] + xb[3])

    wait_grad[lz]()

    @pl.when(x % 2 == 0)
    def _():
        upper = tx[0][1]
        for n in range(3, X, 2):
            upper = jnp.where(x == n - 1, tx[0][n], upper)
        acc = zb[0, lz]
        for p in range(1, Z):
            acc = acc + zb[p, lz]
        gp[...] = gp[...] * wide(jnp.exp(upper)) + acc

    grad = gp[...]
    for slot in reversed(range(1, lz)):
        wait_grad[slot]()
    grads = [grad]
    for i in reversed(range(lz)):
        deeper = []
        for n in range(Z >> i):
            above = grads[n // 2]
            if n % 2 == 0:
                above = above * z_decay[i][n + 1]
                for m in range(1 << i if i else 0):
                    above = above + zb[((n + 1) << i) + m, i]
            deeper.append(above)
        grads = deeper
    for n in range(Z):
        g1s[n] = grads[n]
    wait_own_grad = exchange(
        z_links, lambda p: g1s.at[p], lambda p: g1.at[rows(k * half + p * SR, SR)], slices)
    g1[rows(k * half + z * SR, SR), :] = g1s[z]

    def own_chunk(part, received, own):
        received[y] = part[rows(y * chunk, chunk), :]
        acc = received[0]
        for p in range(1, Y):
            acc = acc + received[p]
        own[...] = left_three(acc, order)

    wait_read_parts()
    own_chunk(part_r, rs_r, own_r)
    wait_read = exchange(
        y_links, lambda p: own_r, lambda p: gr_ref.at[rows(p * chunk, chunk)],
        lambda n: rs_r.at[0:n])
    gr_ref[rows(y * chunk, chunk), :] = own_r[...]

    wait_own_grad()
    wait_grad[0]()

    @pl.when(z % 2 == 0)
    def _():
        g1[mine, :] = g1[mine, :] + d1[...]

    wait_half_grad = exchange(
        core_links, lambda p: g1.at[mine], lambda p: g1.at[rows(p * half, half)],
        lambda n: s1h)
    wait_lowest()
    wait_half_grad()

    end_grad = g1[...] * from_own + d0[...]
    end_high, end_low = split(end_grad)
    part_w[...] = part_w[...] + (
        mul(fh[...], end_high, NT) + (mul(fl[...], end_high, NT) + mul(fh[...], end_low, NT)))
    wait_write_parts = exchange(
        y_links, lambda p: part_w.at[rows(p * chunk, chunk)], lambda p: rs_w.at[p],
        lambda n: rs_w.at[0:n])
    pulled_all = gl_ref[2]
    for depth in range(1, cross):
        pulled_all = pulled_all + gl_ref[2 + depth]
    passing = jnp.sum(pulled_all, axis=1, keepdims=True)
    line = jnp.sum(own_e[...] * end_grad, axis=0, keepdims=True)
    change = jnp.sum(jnp.where(pick, line, 0.0), axis=1, keepdims=True) - passing
    v_own[...] = jnp.broadcast_to(change, (H, 128))
    wait_change = exchange(core_links, lambda p: v_own, lambda p: v_core, lambda n: v_core)
    wait_change()
    v_pair[...] = v_own[...] + v_core[...]
    wait_changes = exchange(
        z_links, lambda p: v_pair, lambda p: v_z.at[p], lambda n: v_z.at[0:n])
    spread = mul(write_p, end_high) + mul(write_p, end_low)
    gv_ref[...] = (gvl[...] + spread * fx[...]).astype(BF16)
    store(gv_ref, gv_out)
    fade_pull = right_two(pick16, fd[...] * spread, NT)
    within = exact(pulled_all + gsm[...], jnp.where(t_row >= t_col, 1.0, 0.0))
    within = within + exact(fade_pull, jnp.where(t_row < t_col, 1.0, 0.0)) - passing
    wait_read()
    store(gr_ref, gr_out)

    wait_write_parts()
    own_chunk(part_w, rs_w, own_w)
    wait_write = exchange(
        y_links, lambda p: own_w, lambda p: gw_ref.at[rows(p * chunk, chunk)],
        lambda n: rs_w.at[0:n])
    gw_ref[rows(y * chunk, chunk), :] = own_w[...]

    passed = jnp.where(k == 1, v_core[...], 0.0)
    wait_changes()
    v_z[z] = v_pair[...]
    in_plane = jnp.zeros((H, 128), F32)
    for p in range(Z):
        tile = v_z[p]
        in_plane = in_plane + tile
        passed = passed + jnp.where(z > p, tile, 0.0)
    v_plane[...] = in_plane
    wait_plane_changes = exchange(
        x_links, lambda p: v_plane, lambda p: v_x.at[p], lambda n: v_x.at[0:n])
    wait_plane_changes()
    v_x[x] = in_plane
    for p in range(X):
        passed = passed + jnp.where(x > p, v_x[p], 0.0)
    gd_ref[...] = within + passed[:, 0:1]
    store(gd_ref, gd_out)
    wait_write()
    store(gw_ref, gw_out)
    for item in stores:
        item.wait()

    for wait_sent in sent:
        wait_sent()


def copy_out(count, *refs):
    sources, targets, held = (refs[n * count:(n + 1) * count] for n in range(3))
    sems = refs[3 * count]
    loads = [
        pltpu.make_async_copy(sources[n], held[n], sems.at[0, n]) for n in range(count)
    ]
    stores = [
        pltpu.make_async_copy(held[n], targets[n], sems.at[1, n]) for n in range(count)
    ]
    for item in loads:
        item.start()
    for load, item in zip(loads, stores):
        load.wait()
        item.start()
    for item in stores:
        item.wait()


def shards(X, Z, Y, values, gate, write, read, decay, logit, gain, cot, final_cot):
    T, C = values.shape
    N = write.shape[1]
    H = decay.shape[0]
    width = C // H
    SR = 2 * X
    half = Z * SR
    lz, lx = Z.bit_length() - 1, X.bit_length() - 1
    slots = lz + lx
    cross = 1 + slots
    chunk = T // Y

    def mem(*shape, dtype=F32):
        return pltpu.VMEM(shape, dtype)

    sem = pltpu.SemaphoreType.DMA
    outs = (
        ((T, C), BF16), ((T, C), BF16), ((T, C), BF16), ((T, N), F32), ((T, N), F32),
        ((H, T), F32), (logit.shape, F32), (final_cot.shape, F32),
    )
    args = (values, gate, write, read, decay, logit, gain.reshape(1, C), cot, final_cot)
    scratch = dict(
        fx=mem(T, C), fd=mem(T, C), fh=mem(T, C, dtype=BF16), fl=mem(T, C, dtype=BF16),
        silu_=mem(T, C), slope=mem(T, C), ss=mem(T, C), s2=mem(T, C), cols=mem(T, 128),
        go=mem(T, C), rt=mem(N, T, dtype=BF16), gh=mem(T, C, dtype=BF16),
        gl2=mem(T, C, dtype=BF16), own_e=mem(N, C), core_e=mem(N, C),
        s1h=mem(half, C), s1t=mem(Z, SR, C + 128), zr=mem(Z, SR, C + 128), zs=mem(Z - 1, SR, C),
        plane_t=mem(SR, C + 128), xr=mem(X, SR, C + 128), xs=mem(X - 1, SR, C), st=mem(slots, N, C),
        wx=mem(cross, T, C), wp=mem(cross, T, C), md=mem(H, T, T), ya=mem(T, C),
        dl=mem(cross, N, C), dr=mem(slots, half, C), d0=mem(N, C), dh=mem(slots, half, C),
        zb=mem(Z, slots, SR, C), d1=mem(half, C), xbs=mem(SR, C), xb=mem(X, SR, C),
        gp=mem(SR, C), g1s=mem(Z, SR, C), g1=mem(N, C), gsc=mem(T, T), gvl=mem(T, C), gsm=mem(H, T),
        t_own=mem(H, 128), t_core=mem(H, 128), f_own=mem(H, 128), f_x=mem(X, H, 128),
        v_own=mem(H, 128), v_core=mem(H, 128), v_pair=mem(H, 128), v_z=mem(Z, H, 128),
        v_plane=mem(H, 128), v_x=mem(X, H, 128),
        n_own=mem(8, T), n_y=mem(Y, 8, T),
        part_r=mem(T, N), rs_r=mem(Y, chunk, N), own_r=mem(chunk, N),
        part_w=mem(T, N), rs_w=mem(Y, chunk, N), own_w=mem(chunk, N),
        send_sems=sem((24 + 4 * slots,)), recv_sems=sem((24 + 4 * slots,)),
        in_sems=sem((9,)), out_sems=sem((8,)),
    )
    anywhere = pl.BlockSpec(memory_space=pl.ANY)
    results = pl.pallas_call(
        functools.partial(layer, (X, Z, Y, T, N, H, width)),
        out_shape=tuple(jax.ShapeDtypeStruct(shape, dtype) for shape, dtype in outs),
        in_specs=[anywhere] * len(args),
        out_specs=(anywhere,) * len(outs),
        scratch_shapes=(
            [mem(*a.shape, dtype=a.dtype) for a in args]
            + [mem(*shape, dtype=dtype) for shape, dtype in outs] + list(scratch.values())),
        compiler_params=pltpu.CompilerParams(
            collective_id=0, has_side_effects=True, vmem_limit_bytes=56 * 2**20
        ),
    )(*args)
    return pl.pallas_call(
        functools.partial(copy_out, len(results)),
        out_shape=tuple(jax.ShapeDtypeStruct(shape, dtype) for shape, dtype in outs),
        in_specs=[anywhere] * len(results),
        out_specs=(anywhere,) * len(results),
        scratch_shapes=(
            [mem(*shape, dtype=dtype) for shape, dtype in outs] + [sem((2, len(results)))]),
        compiler_params=pltpu.CompilerParams(vmem_limit_bytes=56 * 2**20),
    )(*results)


def solution(mesh):
    ctx, heads = mesh.shape["ctx"], mesh.shape["head"]
    X = 1 << ((ctx.bit_length() - 2) // 2)
    Z = ctx // 2 // X
    return jax.shard_map(
        functools.partial(shards, X, Z, heads),
        mesh=mesh,
        in_specs=(
            P("ctx", "head"),
            P("ctx", "head"),
            P("ctx", None),
            P("ctx", None),
            P("head", "ctx"),
            P(None, "head", "ctx"),
            P("head"),
            P("ctx", "head"),
            P("head", "ctx"),
        ),
        out_specs=(
            P("ctx", "head"),
            P("ctx", "head"),
            P("ctx", "head"),
            P("ctx", None),
            P("ctx", None),
            P("head", "ctx"),
            P(None, "head", "ctx"),
            P("head", "ctx"),
        ),
        check_vma=False,
    )
```

```python
import functools

import jax
import jax.numpy as jnp
from jax import lax
from jax.experimental import pallas as pl
from jax.experimental.pallas import tpu as pltpu
from jax.sharding import PartitionSpec as P

F32 = jnp.float32
BF16 = jnp.bfloat16
EPSILON = 1e-05
BLOCK = 64
FAR = -1e30
NN = (((1,), (0,)), ((), ()))
NT = (((1,), (1,)), ((), ()))
TN = (((0,), (0,)), ((), ()))


def split(array):
    high = array.astype(BF16)
    return high, (array - high.astype(F32)).astype(BF16)


def mul(a, b, dims=NN):
    return lax.dot_general(a, b, dims, preferred_element_type=F32)


def left_two(a, b, dims=NN):
    high, low = split(a)
    return mul(high, b, dims) + mul(low, b, dims)


def right_two(a, b, dims=NN):
    high, low = split(b)
    return mul(a, high, dims) + mul(a, low, dims)


def both(a, b, dims=NN):
    a_high, a_low = split(a)
    b_high, b_low = split(b)
    return mul(a_high, b_high, dims) + (mul(a_low, b_high, dims) + mul(a_high, b_low, dims))


def exact(a, b, dims=NN):
    return lax.dot_general(
        a, b, dims, precision=lax.Precision.HIGHEST, preferred_element_type=F32
    )


def left_three(a, b, dims=NN):
    high = a.astype(BF16)
    rest = a - high.astype(F32)
    middle, low = split(rest)
    return mul(high, b, dims) + (mul(middle, b, dims) + mul(low, b, dims))


def iota(shape, dim):
    return lax.broadcasted_iota(jnp.int32, shape, dim)


def far_first(count):
    return sorted(range(1, count), key=lambda j: -min(j, count - j))


def layer(
    sizes,
    v_in, g_in, b_in, r_in, ld_in, ll_in, gain_in, ct_in, fc_in,
    mixed_out, gv_out, gg_out, gw_out, gr_out, gd_out, gl_out, fs_out,
    v_ref, g_ref, b_ref, r_ref, ld_ref, ll_ref, gain_ref, ct_ref, fc_ref,
    mixed_ref, gv_ref, gg_ref, gw_ref, gr_ref, gd_ref, gl_ref, fs_ref,
    fx, fd, fh, fl, silu_, slope, ss, s2, cols, go, rt, gh, gl2, own_e, core_e, s1h, s1t, zr, zs, plane_t, xr, xs, st,
    wx, wp, md, ya, dl, dr, d0, dh, zb, d1, xbs, xb, gp, g1s, g1, gsc, gvl, gsm,
    t_own, t_core, f_own, f_x,
    v_own, v_core, v_pair, v_z, v_plane, v_x,
    n_own, n_y, part_r, rs_r, own_r, part_w, rs_w, own_w,
    send_sems, recv_sems, in_sems, out_sems,
):
    X, Z, Y, T, N, H, width = sizes
    C = H * width
    SR = 2 * X
    half = Z * SR
    lz, lx = Z.bit_length() - 1, X.bit_length() - 1
    cross = 1 + lz + lx
    slots = lz + lx
    final_scale = (N / (T * X * Z * 2)) ** 0.5
    channels = C * Y

    me = lax.axis_index("ctx")
    y = lax.axis_index("head")
    k = me % 2
    z = (me // 2) % Z
    x = me // (2 * Z)
    kf = k.astype(F32)

    def device(x_, z_, k_, y_):
        return (x_ * (2 * Z) + z_ * 2 + k_, y_)

    core_links = (k, [(1 - k, device(x, z, 1 - k, y))])
    z_links = (z, [(p, device(x, p, k, y)) for p in [(z + j) % Z for j in far_first(Z)]])
    x_links = (x, [(p, device(p, z, k, y)) for p in [(x + j) % X for j in far_first(X)]])
    y_links = (y, [(p, device(x, z, k, p)) for p in [(y + j) % Y for j in far_first(Y)]])
    z_pair = z + 1 - 2 * (z % 2)
    pair_links = (0, [(0, device(x, z_pair, k, y))])
    all_z = [(z + j) % Z for j in far_first(Z) + [0]]

    def plane_links(plane):
        return (z, [(p, device(plane, p, k, y)) for p in all_z])

    next_plane = x + 1 - 2 * (x % 2)
    mirror_plane = X - 1 - x

    barrier = pltpu.get_barrier_semaphore()
    lines = [(z_links, Z), (y_links, Y), (x_links, X), (core_links, 2)]
    peers = [
        (-min(j, size - j), dev)
        for links, size in lines for j, (_, dev) in zip(far_first(size), links[1])]
    peers = [dev for _, dev in sorted(peers, key=lambda pair: pair[0])]
    for peer in peers:
        pl.semaphore_signal(barrier, inc=1, device_id=peer, device_id_type=pl.DeviceIdType.MESH)

    loads = {}
    for n, (name, src, dst) in enumerate((
        ("ld", ld_in, ld_ref), ("b", b_in, b_ref), ("v", v_in, v_ref), ("fc", fc_in, fc_ref),
        ("r", r_in, r_ref), ("ll", ll_in, ll_ref), ("g", g_in, g_ref),
        ("gain", gain_in, gain_ref), ("ct", ct_in, ct_ref),
    )):
        loads[name] = pltpu.make_async_copy(src, dst, in_sems.at[n])
        loads[name].start()
    stores = []

    def store(src, dst):
        item = pltpu.make_async_copy(src, dst, out_sems.at[len(stores)])
        item.start()
        stores.append(item)

    sent = []

    def do(cond, action):
        if cond is None:
            action()
        else:
            pl.when(cond)(action)

    def exchange(links, src_of, dst_of, whole, send_if=lambda p: None, gone=None, got=None):
        mine_, others = links
        index = len(sent)
        everyone = [(None, len(others))]

        def item(src, dst, device_id):
            return pltpu.make_async_remote_copy(
                src_ref=src, dst_ref=dst, send_sem=send_sems.at[index],
                recv_sem=recv_sems.at[index], device_id=device_id,
                device_id_type=pl.DeviceIdType.MESH,
            )

        for p, device_id in others:
            do(send_if(p), item(src_of(p), dst_of(mine_), device_id).start)

        def wait_all(counts, kind):
            for cond, count in counts:
                if count:
                    ref = whole(count)
                    do(cond, getattr(item(ref, ref, others[0][1]), kind))

        sent.append(lambda: wait_all(gone or everyone, "wait_send"))

        def wait():
            wait_all(got or everyone, "wait_recv")

        return wait

    def slices(count):
        return g1s.at[0:count]

    def half_of(condition):
        return [(condition, Z // 2 - 1), (jnp.logical_not(condition), Z // 2)]

    def bit(index, place):
        return (index // 2**place) % 2 == 1

    def needs(z_, slot):
        return bit(z_, slot) if slot < lz else bit(x, slot - lz)

    def rows(start, size):
        return pl.ds(pl.multiple_of(start, size), size)

    head_of = iota((H, C), 1) // width
    pick = head_of == iota((H, C), 0)
    pick16 = jnp.where(pick, 1.0, 0.0).astype(BF16)

    def wide(tile):
        many = jnp.concatenate([tile] * (C // 128), axis=1)
        return jnp.sum(jnp.where(pick, many, 0.0), axis=0, keepdims=True)

    def spread_out(array):
        return left_two(array, pick16, TN)

    j_ = iota((N, N), 0)
    n_ = iota((N, N), 1)
    natural = ((j_ % SR) // 2) * (4 * Z) + ((j_ % half) // SR) * 4 + (j_ // half) * 2 + j_ % 2
    order = jnp.where(natural == n_, 1.0, 0.0).astype(BF16)


    t_row = iota((T, T), 0)
    t_col = iota((T, T), 1)
    upto = jnp.where(t_row <= t_col, 1.0, 0.0)
    loads["ld"].wait()
    cum = exact(ld_ref[...], upto)
    total = jnp.broadcast_to(cum[:, T - 1:T], (H, 128))
    t_own[...] = total
    fade = jnp.exp(cum[:, T - 1:T] - cum)
    fx[...] = spread_out(fade)
    loads["b"].wait()
    write = b_ref[...]
    write_t = mul(order, write, NT).astype(BF16)
    loads["v"].wait()
    faded = v_ref[...].astype(F32) * fx[...]
    fd[...] = faded
    own_e[...] = right_two(write_t, faded)
    loads["fc"].wait()
    f_own[...] = fc_ref[...]

    @pl.when(k == 1)
    def _():
        d0[...] = jnp.zeros((N, C), F32)

    pl.semaphore_wait(barrier, len(peers))

    wait_total = exchange(core_links, lambda p: t_own, lambda p: t_core, lambda n: t_core)
    wait_end = exchange(
        core_links, lambda p: own_e.at[rows(p * half, half)],
        lambda p: core_e.at[rows((1 - p) * half, half)], lambda n: s1h)
    wait_total()
    upper_total = jnp.where(k == 1, t_own[...], t_core[...])
    upper_decay = wide(jnp.exp(upper_total))
    from_own = kf + (1.0 - kf) * upper_decay
    from_core = (1.0 - kf) + kf * upper_decay
    mine = rows(k * half, half)
    chip_total = t_own[...] + t_core[...]
    for n in range(Z):
        s1t[n, :, C:] = chip_total

    wait_end()
    merged = own_e[mine, :] * from_own + core_e[mine, :] * from_core
    for n in range(Z):
        s1t[n, :, :C] = merged[n * SR:(n + 1) * SR, :]
    wait_slices = exchange(
        z_links, lambda p: s1t.at[p], lambda p: zr.at[p], lambda n: zr.at[0:n])
    s1h[...] = merged
    wait_state = [None] * slots
    wait_half = [None] * slots
    wait_final = exchange(
        x_links, lambda p: f_own, lambda p: f_x.at[p], lambda n: f_x.at[0:n])
    wait_state[0] = exchange(
        pair_links, lambda p: s1h, lambda p: st.at[0, mine], lambda n: s1h,
        lambda p: z % 2 == 0, [(z % 2 == 0, 1)], [(z % 2 == 1, 1)])
    zr[z] = s1t[z]
    wait_other_end = exchange(
        core_links, lambda p: own_e.at[0:half], lambda p: core_e.at[0:half], lambda n: s1h,
        lambda p: k == 0, [(k == 0, 1)], [(k == 1, 1)])

    loads["r"].wait()
    read = r_ref[...]
    write_p = mul(write, order, NT).astype(BF16)
    read_p = mul(read, order, NT).astype(BF16)
    read_t = mul(order, read, NT).astype(BF16)
    rt[...] = read_t
    scores = mul(read, write, NT)
    loads["ll"].wait()
    cum_t = jnp.transpose(jnp.concatenate(
        [cum, ll_ref[0], ll_ref[1], jnp.zeros((128 - 3 * H, T), F32)], axis=0))
    later = t_row >= t_col
    same = (t_row // BLOCK) == (t_col // BLOCK)
    lane = iota((T, 128), 1)
    left = lane < width

    def head_mix(h):
        logit = jnp.where(same, cum_t[:, H + h:H + h + 1], cum_t[:, 2 * H + h:2 * H + h + 1])
        power = cum_t[:, h:h + 1] - cum[h:h + 1, :] + logit
        return jnp.exp(jnp.where(later, power, FAR))

    def local_pair(pair):
        vals = v_ref[:, pair * 128:(pair + 1) * 128]
        zero = jnp.zeros_like(vals)
        blocks = jnp.concatenate(
            [jnp.where(left, vals, zero), jnp.where(left, zero, vals)], axis=0)
        kernels = []
        for h in (2 * pair, 2 * pair + 1):
            mix = head_mix(h)
            md[h] = mix
            kernels.append(mix * scores)
        ya[:, pair * 128:(pair + 1) * 128] = left_two(
            jnp.concatenate(kernels, axis=1), blocks)

    local_pair(0)

    local_pair(1)

    wait_slices()

    def tree_totals(tiles):
        levels = [tiles]
        while len(levels[-1]) > 1:
            last = levels[-1]
            levels.append([last[n] + last[n + 1] for n in range(0, len(last), 2)])
        decays = [
            [wide(jnp.exp(tile)) if n % 2 else None for n, tile in enumerate(level)]
            for level in levels[:-1]]
        return levels, decays

    tz, z_decay = tree_totals([zr[n, :, C:] for n in range(Z)])
    z_nodes = [zr]
    base = 0
    for i in range(lz):
        here = z_nodes[i]
        count = Z >> (i + 1)
        there = zs.at[base:base + count]
        for n in range(count):
            there[n] = here[2 * n, :, :C] * z_decay[i][2 * n + 1] + here[2 * n + 1, :, :C]
        z_nodes.append(there)
        base += count

    plane = z_nodes[lz].at[0]
    plane_t[:, :C] = plane[...]
    plane_t[:, C:] = tz[lz][0]
    wait_planes = exchange(
        x_links, lambda p: plane_t, lambda p: xr.at[p], lambda n: xr.at[0:n])
    xr[x] = plane_t[...]

    def slice_of(slot):
        return lambda p: st.at[slot, rows(k * half + p * SR, SR)]

    wait_final()
    wait_state[lz] = exchange(
        plane_links(next_plane), lambda p: plane, slice_of(lz), slices,
        lambda p: x % 2 == 0, [(x % 2 == 0, Z)], [(x % 2 == 1, Z)])
    for i in reversed(range(1, lz)):
        def below(p, i=i):
            return z_nodes[i].at[jnp.maximum(p // 2**i - 1, 0)]

        wait_state[i] = exchange(
            z_links, below, slice_of(i), slices, lambda p: bit(p, i),
            half_of(bit(z, i)), [(bit(z, i), Z - 1)])

        @pl.when(bit(z, i))
        def _():
            st[i, rows(k * half + z * SR, SR), :] = below(z)[...]

    def from_core_too(slot):
        wait_state[slot]()
        wait_half[slot] = exchange(
            core_links, lambda p: st.at[slot, mine], lambda p: st.at[slot, rows(p * half, half)],
            lambda n: s1h, lambda p: needs(z, slot), [(needs(z, slot), 1)],
            [(needs(z, slot), 1)])

    local_pair(2)
    from_core_too(0)

    wait_planes()
    tx, x_decay = tree_totals([xr[n, :, C:] for n in range(X)])
    x_nodes = [xr]
    base = 0
    for i in range(lx):
        here = x_nodes[i]
        count = X >> (i + 1)
        there = xs.at[base:base + count]
        for n in range(count):
            there[n] = here[2 * n, :, :C] * x_decay[i][2 * n + 1] + here[2 * n + 1, :, :C]
        x_nodes.append(there)
        base += count
    if lx > 1:
        lower = x_nodes[1].at[0]
        wait_cross = exchange(
            plane_links(mirror_plane), lambda p: lower, slice_of(lz + 1), slices,
            lambda p: x == 1, [(x == 1, Z)], [(x == 2, Z)])
        wait_inside = exchange(
            z_links, lambda p: lower, slice_of(lz + 1), slices,
            lambda p: x == 3, [(x == 3, Z - 1)], [(x == 3, Z - 1)])

        @pl.when(x == 3)
        def _():
            st[lz + 1, rows(k * half + z * SR, SR), :] = lower[...]

        def wait_both():
            wait_cross()
            wait_inside()

        wait_state[lz + 1] = wait_both

    local_pair(3)

    offset = jnp.zeros((H, 128), F32)
    for depth in range(cross):
        wx[depth] = spread_out(jnp.exp(ll_ref[2 + depth] + (offset + cum)))
        if depth == 0:
            offset = offset + jnp.where(k == 1, t_core[...], 0.0)
        elif depth <= lz:
            i = depth - 1
            for n in range(0, Z >> i, 2):
                offset = offset + jnp.where(z // 2**i == n + 1, tz[i][n], 0.0)
        else:
            i = depth - 1 - lz
            for n in range(0, X >> i, 2):
                offset = offset + jnp.where(x // 2**i == n + 1, tx[i][n], 0.0)

    def read_level(depth, state):
        weighted = wx[depth] * right_two(read_p, state[...])
        wp[depth] = weighted
        ya[...] = ya[...] + weighted

    def read_slot(slot):
        wait_half[slot]()

        @pl.when(needs(z, slot))
        def _():
            read_level(1 + slot, st.at[slot])

    wait_other_end()

    @pl.when(k == 1)
    def _():
        read_level(0, core_e)

    read_slot(0)

    whole = x_nodes[lx][0] * final_scale
    slice_row = iota((SR, C), 0)
    tile_lane = iota((H, 128), 1)

    def narrow(index):
        line = jnp.sum(jnp.where(slice_row == index, whole, 0.0), axis=0, keepdims=True)
        masked = jnp.where(pick, line, 0.0)
        tile = masked[:, 0:128]
        for n in range(1, C // 128):
            tile = tile + masked[:, n * 128:(n + 1) * 128]
        return tile + pltpu.roll(tile, width, 1)

    fs_ref[...] = jnp.where(tile_lane < width, narrow(2 * x), narrow(2 * x + 1))
    store(fs_ref, fs_out)

    loads["g"].wait()
    gate = g_ref[...].astype(F32)
    sigma = jax.nn.sigmoid(gate)
    silu = gate * sigma
    silu_[...] = silu
    s2[...] = silu * silu
    loads["gain"].wait()
    loads["ct"].wait()
    ss[...] = ct_ref[...].astype(F32) * gain_ref[...] * silu
    slope[...] = sigma * (1.0 + gate * (1.0 - sigma))
    faded_high, faded_low = split(fd[...])
    fh[...] = faded_high
    fl[...] = faded_low

    for slot in list(range(lz - 1, 0, -1)) + list(range(lz, slots)):
        from_core_too(slot)
        if slot < lz:
            read_slot(slot)
    for slot in range(lz, slots):
        read_slot(slot)

    out = ya[...]

    def folded(array):
        tile = array[:, 0:128]
        for n in range(1, C // 128):
            tile = tile + array[:, n * 128:(n + 1) * 128]
        return tile

    ones = jnp.ones((8, 128), BF16)
    squares = right_two(ones, folded(out * out * s2[...]), NT)
    inners = right_two(ones, folded(out * ss[...]), NT)
    n_own[...] = jnp.where(iota((8, T), 0) == 0, squares, inners)
    wait_norm = exchange(
        y_links, lambda p: n_own, lambda p: n_y.at[p], lambda n: n_y.at[0:n])
    n_y[y] = n_own[...]
    wait_norm()
    sums = n_y[0]
    for p in range(1, Y):
        sums = sums + n_y[p]
    inverse = lax.rsqrt(sums[0:1, :] / channels + EPSILON)
    turn = inverse * inverse * (inverse * sums[1:2, :] / channels)
    cols[...] = jnp.transpose(
        jnp.concatenate([inverse, turn, jnp.zeros((126, T), F32)], axis=0))
    go[...] = cols[:, 0:1] * ss[...] - cols[:, 1:2] * (out * s2[...])

    def state_grad(depth):
        dl[depth] = right_two(read_t, go[...] * wx[depth])

    def half_grad(depth, part):
        read_half = rt[part, :]
        dl[depth, part, :] = mul(read_half, gh[...]) + mul(read_half, gl2[...])

    wait_core_grad = [None] * slots
    wait_grad = [None] * slots
    other = rows((1 - k) * half, half)

    def start_slot(slot):
        @pl.when(needs(z, slot))
        def _():
            high, low = split(go[...] * wx[1 + slot])
            gh[...] = high
            gl2[...] = low
            half_grad(1 + slot, other)

        wait_core_grad[slot] = exchange(
            core_links, lambda p: dl.at[1 + slot, rows(p * half, half)], lambda p: dr.at[slot],
            lambda n: s1h, lambda p: needs(z, slot), [(needs(z, slot), 1)],
            [(needs(z, slot), 1)])

        @pl.when(needs(z, slot))
        def _():
            half_grad(1 + slot, mine)

    def finish_slot(slot):
        wait_core_grad[slot]()

        @pl.when(needs(z, slot))
        def _():
            dh[slot] = dl[1 + slot, mine, :] + dr[slot]

        def piece(p):
            return dh.at[slot, rows(p * SR, SR)]

        if slot == 0:
            wait_grad[0] = exchange(
                pair_links, lambda p: dh.at[0], lambda p: d1, lambda n: s1h,
                lambda p: z % 2 == 1, [(z % 2 == 1, 1)], [(z % 2 == 0, 1)])
        elif slot == lz:
            wait_grad[slot] = exchange(
                plane_links(next_plane), piece, lambda p: zb.at[p, slot], slices,
                lambda p: x % 2 == 1, [(x % 2 == 1, Z)], [(x % 2 == 0, Z)])
        else:
            wait_grad[slot] = exchange(
                z_links, piece, lambda p: zb.at[p, slot], slices,
                lambda p: needs(z, slot), [(needs(z, slot), Z - 1)],
                half_of(bit(z, slot)) if slot < lz else [(needs(z, slot), Z - 1)])

            @pl.when(needs(z, slot))
            def _():
                zb[z, slot] = piece(z)[...]

    for slot in reversed(range(slots)):
        start_slot(slot)
        if slot + 1 < slots:
            finish_slot(slot + 1)

    @pl.when(k == 1)
    def _():
        state_grad(0)

    finish_slot(0)
    wait_lowest = exchange(
        core_links, lambda p: dl.at[0], lambda p: d0, lambda n: core_e,
        lambda p: k == 1, [(k == 1, 1)], [(k == 0, 1)])

    inverse, turn = cols[:, 0:1], cols[:, 1:2]
    gated = ya[...] * silu_[...]
    gain = gain_ref[...]
    mixed_ref[...] = (gated * inverse * gain).astype(BF16)
    store(mixed_ref, mixed_out)
    grad_gated = inverse * (ct_ref[...].astype(F32) * gain) - turn * gated
    gg_ref[...] = (grad_gated * ya[...] * slope[...]).astype(BF16)
    store(gg_ref, gg_out)

    gsc[...] = jnp.zeros((T, T), F32)
    block_pick = jnp.where(
        iota((8, T), 0) == iota((8, T), 1) // BLOCK, 1.0, 0.0).astype(BF16)
    late = iota((1, T), 1) >= BLOCK

    def backward_pair(pair):
        lanes = slice(pair * 128, (pair + 1) * 128)
        vals = v_ref[:, lanes]
        grads = go[:, lanes]
        zero = jnp.zeros_like(grads)
        parts = [jnp.where(left, grads, zero), jnp.where(left, zero, grads)]
        kernels = []
        for h, part in zip((2 * pair, 2 * pair + 1), parts):
            mix = md[h]
            kernel = mix * scores
            kernels.append(kernel)
            pull = left_two(part, vals, NT)
            gsc[...] = gsc[...] + pull * mix
            pulled = pull * kernel
            sums = right_two(block_pick, pulled, NT)
            first, second = sums[0:1, :], sums[1:2, :]
            gl_ref[0, h:h + 1, :] = jnp.where(late, second, first)
            gl_ref[1, h:h + 1, :] = jnp.where(late, first, 0.0)
            gsm[h:h + 1, :] = first + second - jnp.sum(pulled, axis=0, keepdims=True)
        gvl[:, lanes] = both(
            jnp.concatenate(kernels, axis=0), jnp.concatenate(parts, axis=0), TN)

    backward_pair(0)
    backward_pair(1)

    if lx > 1:
        wait_grad[lz + 1]()

        @pl.when(x >= 2)
        def _():
            acc = zb[0, lz + 1]
            for p in range(1, Z):
                acc = acc + zb[p, lz + 1]
            xbs[...] = acc

        wait_plane_grads = exchange(
            x_links, lambda p: xbs, lambda p: xb.at[p], slices,
            lambda p: jnp.logical_and(x >= 2, p < 2), [(x >= 2, 2)], [(x < 2, 2)])

    backward_pair(2)
    backward_pair(3)

    part_r[...] = left_two(gsc[...], write_p)
    part_w[...] = left_two(gsc[...], read_p, TN)
    pulled_all = jnp.zeros((H, T), F32)

    def level_back(depth, state):
        weighted = go[...] * wx[depth]
        part_r[...] = part_r[...] + both(weighted, state[...], NT)
        gl_ref[2 + depth] = right_two(pick16, go[...] * wp[depth], NT)

    for depth in range(cross):
        cond = (k == 1) if depth == 0 else needs(z, depth - 1)

        @pl.when(cond)
        def _():
            level_back(depth, core_e if depth == 0 else st.at[depth - 1])

        @pl.when(jnp.logical_not(cond))
        def _():
            gl_ref[2 + depth] = jnp.zeros((H, T), F32)

    store(gl_ref, gl_out)

    chunk = T // Y
    wait_read_parts = exchange(
        y_links, lambda p: part_r.at[rows(p * chunk, chunk)], lambda p: rs_r.at[p],
        lambda n: rs_r.at[0:n])

    f_x[x] = f_own[...]
    grad = jnp.zeros((SR, C), F32)
    for n in range(X):
        tile = f_x[n]
        turned = pltpu.roll(tile, width, 1)
        grad = jnp.where(slice_row == 2 * n, wide(jnp.where(tile_lane < width, tile, turned)), grad)
        grad = jnp.where(
            slice_row == 2 * n + 1, wide(jnp.where(tile_lane < width, turned, tile)), grad)
    grad = grad * final_scale

    gp[...] = grad
    if lx > 1:
        wait_plane_grads()

        @pl.when(x < 2)
        def _():
            gp[...] = gp[...] * x_decay[1][1] + (xb[2] + xb[3])

    wait_grad[lz]()

    @pl.when(x % 2 == 0)
    def _():
        upper = tx[0][1]
        for n in range(3, X, 2):
            upper = jnp.where(x == n - 1, tx[0][n], upper)
        acc = zb[0, lz]
        for p in range(1, Z):
            acc = acc + zb[p, lz]
        gp[...] = gp[...] * wide(jnp.exp(upper)) + acc

    grad = gp[...]
    for slot in reversed(range(1, lz)):
        wait_grad[slot]()
    grads = [grad]
    for i in reversed(range(lz)):
        deeper = []
        for n in range(Z >> i):
            above = grads[n // 2]
            if n % 2 == 0:
                above = above * z_decay[i][n + 1]
                for m in range(1 << i if i else 0):
                    above = above + zb[((n + 1) << i) + m, i]
            deeper.append(above)
        grads = deeper
    for n in range(Z):
        g1s[n] = grads[n]
    wait_own_grad = exchange(
        z_links, lambda p: g1s.at[p], lambda p: g1.at[rows(k * half + p * SR, SR)], slices)
    g1[rows(k * half + z * SR, SR), :] = g1s[z]

    def own_chunk(part, received, own):
        received[y] = part[rows(y * chunk, chunk), :]
        acc = received[0]
        for p in range(1, Y):
            acc = acc + received[p]
        own[...] = left_three(acc, order)

    wait_read_parts()
    own_chunk(part_r, rs_r, own_r)
    wait_read = exchange(
        y_links, lambda p: own_r, lambda p: gr_ref.at[rows(p * chunk, chunk)],
        lambda n: rs_r.at[0:n])
    gr_ref[rows(y * chunk, chunk), :] = own_r[...]

    wait_own_grad()
    wait_grad[0]()

    @pl.when(z % 2 == 0)
    def _():
        g1[mine, :] = g1[mine, :] + d1[...]

    wait_half_grad = exchange(
        core_links, lambda p: g1.at[mine], lambda p: g1.at[rows(p * half, half)],
        lambda n: s1h)
    wait_lowest()
    wait_half_grad()

    end_grad = g1[...] * from_own + d0[...]
    end_high, end_low = split(end_grad)
    part_w[...] = part_w[...] + (
        mul(fh[...], end_high, NT) + (mul(fl[...], end_high, NT) + mul(fh[...], end_low, NT)))
    wait_write_parts = exchange(
        y_links, lambda p: part_w.at[rows(p * chunk, chunk)], lambda p: rs_w.at[p],
        lambda n: rs_w.at[0:n])
    pulled_all = gl_ref[2]
    for depth in range(1, cross):
        pulled_all = pulled_all + gl_ref[2 + depth]
    passing = jnp.sum(pulled_all, axis=1, keepdims=True)
    line = jnp.sum(own_e[...] * end_grad, axis=0, keepdims=True)
    change = jnp.sum(jnp.where(pick, line, 0.0), axis=1, keepdims=True) - passing
    v_own[...] = jnp.broadcast_to(change, (H, 128))
    wait_change = exchange(core_links, lambda p: v_own, lambda p: v_core, lambda n: v_core)
    wait_change()
    v_pair[...] = v_own[...] + v_core[...]
    wait_changes = exchange(
        z_links, lambda p: v_pair, lambda p: v_z.at[p], lambda n: v_z.at[0:n])
    spread = mul(write_p, end_high) + mul(write_p, end_low)
    gv_ref[...] = (gvl[...] + spread * fx[...]).astype(BF16)
    store(gv_ref, gv_out)
    fade_pull = right_two(pick16, fd[...] * spread, NT)
    within = exact(pulled_all + gsm[...], jnp.where(t_row >= t_col, 1.0, 0.0))
    within = within + exact(fade_pull, jnp.where(t_row < t_col, 1.0, 0.0)) - passing
    wait_read()
    store(gr_ref, gr_out)

    wait_write_parts()
    own_chunk(part_w, rs_w, own_w)
    wait_write = exchange(
        y_links, lambda p: own_w, lambda p: gw_ref.at[rows(p * chunk, chunk)],
        lambda n: rs_w.at[0:n])
    gw_ref[rows(y * chunk, chunk), :] = own_w[...]

    passed = jnp.where(k == 1, v_core[...], 0.0)
    wait_changes()
    v_z[z] = v_pair[...]
    in_plane = jnp.zeros((H, 128), F32)
    for p in range(Z):
        tile = v_z[p]
        in_plane = in_plane + tile
        passed = passed + jnp.where(z > p, tile, 0.0)
    v_plane[...] = in_plane
    wait_plane_changes = exchange(
        x_links, lambda p: v_plane, lambda p: v_x.at[p], lambda n: v_x.at[0:n])
    assert len(sent) == send_sems.shape[0]
    settled, stored = len(sent) - 2, len(stores)
    for wait_sent in sent[:settled]:
        wait_sent()
    for item in stores:
        item.wait()
    wait_plane_changes()
    v_x[x] = in_plane
    for p in range(X):
        passed = passed + jnp.where(x > p, v_x[p], 0.0)
    gd_ref[...] = within + passed[:, 0:1]
    store(gd_ref, gd_out)
    wait_write()
    store(gw_ref, gw_out)
    for wait_sent in sent[settled:]:
        wait_sent()
    for item in stores[stored:]:
        item.wait()


def copy_out(count, *refs):
    sources, targets, held = (refs[n * count:(n + 1) * count] for n in range(3))
    sems = refs[3 * count]
    loads = [
        pltpu.make_async_copy(sources[n], held[n], sems.at[0, n]) for n in range(count)
    ]
    stores = [
        pltpu.make_async_copy(held[n], targets[n], sems.at[1, n]) for n in range(count)
    ]
    for item in loads:
        item.start()
    for load, item in zip(loads, stores):
        load.wait()
        item.start()
    for item in stores:
        item.wait()


def shards(X, Z, Y, values, gate, write, read, decay, logit, gain, cot, final_cot):
    T, C = values.shape
    N = write.shape[1]
    H = decay.shape[0]
    width = C // H
    SR = 2 * X
    half = Z * SR
    lz, lx = Z.bit_length() - 1, X.bit_length() - 1
    slots = lz + lx
    cross = 1 + slots
    chunk = T // Y
    exchanges = 18 + 3 * slots + lz + (3 if lx > 1 else 0)

    def mem(*shape, dtype=F32):
        return pltpu.VMEM(shape, dtype)

    sem = pltpu.SemaphoreType.DMA
    outs = (
        ((T, C), BF16), ((T, C), BF16), ((T, C), BF16), ((T, N), F32), ((T, N), F32),
        ((H, T), F32), (logit.shape, F32), (final_cot.shape, F32),
    )
    args = (values, gate, write, read, decay, logit, gain.reshape(1, C), cot, final_cot)
    scratch = dict(
        fx=mem(T, C), fd=mem(T, C), fh=mem(T, C, dtype=BF16), fl=mem(T, C, dtype=BF16),
        silu_=mem(T, C), slope=mem(T, C), ss=mem(T, C), s2=mem(T, C), cols=mem(T, 128),
        go=mem(T, C), rt=mem(N, T, dtype=BF16), gh=mem(T, C, dtype=BF16),
        gl2=mem(T, C, dtype=BF16), own_e=mem(N, C), core_e=mem(N, C),
        s1h=mem(half, C), s1t=mem(Z, SR, C + 128), zr=mem(Z, SR, C + 128), zs=mem(Z - 1, SR, C),
        plane_t=mem(SR, C + 128), xr=mem(X, SR, C + 128), xs=mem(X - 1, SR, C), st=mem(slots, N, C),
        wx=mem(cross, T, C), wp=mem(cross, T, C), md=mem(H, T, T), ya=mem(T, C),
        dl=mem(cross, N, C), dr=mem(slots, half, C), d0=mem(N, C), dh=mem(slots, half, C),
        zb=mem(Z, slots, SR, C), d1=mem(half, C), xbs=mem(SR, C), xb=mem(X, SR, C),
        gp=mem(SR, C), g1s=mem(Z, SR, C), g1=mem(N, C), gsc=mem(T, T), gvl=mem(T, C), gsm=mem(H, T),
        t_own=mem(H, 128), t_core=mem(H, 128), f_own=mem(H, 128), f_x=mem(X, H, 128),
        v_own=mem(H, 128), v_core=mem(H, 128), v_pair=mem(H, 128), v_z=mem(Z, H, 128),
        v_plane=mem(H, 128), v_x=mem(X, H, 128),
        n_own=mem(8, T), n_y=mem(Y, 8, T),
        part_r=mem(T, N), rs_r=mem(Y, chunk, N), own_r=mem(chunk, N),
        part_w=mem(T, N), rs_w=mem(Y, chunk, N), own_w=mem(chunk, N),
        send_sems=sem((exchanges,)), recv_sems=sem((exchanges,)),
        in_sems=sem((9,)), out_sems=sem((8,)),
    )
    anywhere = pl.BlockSpec(memory_space=pl.ANY)
    results = pl.pallas_call(
        functools.partial(layer, (X, Z, Y, T, N, H, width)),
        out_shape=tuple(jax.ShapeDtypeStruct(shape, dtype) for shape, dtype in outs),
        in_specs=[anywhere] * len(args),
        out_specs=(anywhere,) * len(outs),
        scratch_shapes=(
            [mem(*a.shape, dtype=a.dtype) for a in args]
            + [mem(*shape, dtype=dtype) for shape, dtype in outs] + list(scratch.values())),
        compiler_params=pltpu.CompilerParams(
            collective_id=0, has_side_effects=True, vmem_limit_bytes=56 * 2**20
        ),
    )(*args)
    return pl.pallas_call(
        functools.partial(copy_out, len(results)),
        out_shape=tuple(jax.ShapeDtypeStruct(shape, dtype) for shape, dtype in outs),
        in_specs=[anywhere] * len(results),
        out_specs=(anywhere,) * len(results),
        scratch_shapes=(
            [mem(*shape, dtype=dtype) for shape, dtype in outs] + [sem((2, len(results)))]),
        compiler_params=pltpu.CompilerParams(vmem_limit_bytes=56 * 2**20),
    )(*results)


def solution(mesh):
    ctx, heads = mesh.shape["ctx"], mesh.shape["head"]
    X = 1 << ((ctx.bit_length() - 2) // 2)
    Z = ctx // 2 // X
    return jax.shard_map(
        functools.partial(shards, X, Z, heads),
        mesh=mesh,
        in_specs=(
            P("ctx", "head"),
            P("ctx", "head"),
            P("ctx", None),
            P("ctx", None),
            P("head", "ctx"),
            P(None, "head", "ctx"),
            P("head"),
            P("ctx", "head"),
            P("head", "ctx"),
        ),
        out_specs=(
            P("ctx", "head"),
            P("ctx", "head"),
            P("ctx", "head"),
            P("ctx", None),
            P("ctx", None),
            P("head", "ctx"),
            P(None, "head", "ctx"),
            P("head", "ctx"),
        ),
        check_vma=False,
    )
```
